128 devices in a mesh: cuts: 64 (over z, y_hi, x, core), box: 2 (over y_lo).
Axes of the slice: x: 4, y: 4 (y_hi: 2, y_lo: 2; y = y_hi * 2 + y_lo), z: 4, core: 2. Of those that a mesh axis runs over, the one named last changes fastest.
Arguments:
- queries_in: bfloat16 [64, 8, 7, 256], P('cuts', 'box'), may hold values from -6 to 6
- image: bfloat16 [64, 4096, 256], P('cuts', 'box'), may hold values from -6 to 6
- box_coords: int32 [64, 8, 4], P('cuts', 'box'), may hold values from 0 to 1023
- box_mask: int32 [64, 8], P('cuts', 'box'), may hold values from 0 to 1, as said below
- volume_ids: int32 [64], P('cuts'), may hold values from 0 to 31, never falling along the last dimension, each value on 1 to 4 neighbouring positions
- cot_queries: bfloat16 [64, 8, 7, 256], P('cuts', 'box'), may hold values from -6 to 6
- cot_keys: bfloat16 [64, 8, 4096, 256], P('cuts', 'box'), may hold values from -6 to 6
- master: float32 [1579008], P(('cuts', 'box')), may hold values from -32 to 32, as said below
- moment1: float32 [1579008], P(('cuts', 'box')), may hold values from -16384 to 16384, as said below
- moment2: float32 [1579008], P(('cuts', 'box')), may hold values from 0 to 4194304, as said below
Outputs:
- queries_out: bfloat16 [64, 8, 7, 256], P('cuts', 'box')
- keys_out: bfloat16 [64, 8, 4096, 256], P('cuts', 'box')
- queries_grad: float32 [64, 8, 7, 256], P('cuts', 'box')
- image_grad: float32 [64, 4096, 256], P('cuts', 'box')
- new_master: float32 [1579008], P(('cuts', 'box'))
- new_first: float32 [1579008], P(('cuts', 'box'))
- new_second: float32 [1579008], P(('cuts', 'box'))
- new_copy: bfloat16 [1579008], P(('cuts', 'box'))
- matrix_norms: float32 [2, 14], replicated
The draws below stay inside these ranges and needn't reach their ends.
Inputs may be any that keep to these rules, and one draw needn't show every extreme that they name: `box_mask`: every slice has at least two live boxes. `volume_ids`: volume numbers never fall from slice to slice; each volume has one to four slices. `master`: the parameters laid out as the first step states; padding entries are arbitrary. `moment1`: arbitrary real values. `moment2`: positive.
All inputs are finite; a program needn't handle non-finite values.
Results may differ from the reference program's by a relative error of at most 0.0018.
The reference program's roundings to bfloat16 on the way count: a program that leaves them out, or rounds other values in their place, can miss the bound.
Values may be sent and summed in bfloat16 or wider, within the bound.
No kernel may reach another device: no remote copies, remote signals or barrier semaphores. Data moves between devices by JAX's collectives and lax.ppermute only.
A program may use at most 256 MiB of HBM per device.

```python
import math
import jax
import jax.numpy as jnp
import numpy as np
from jax import lax

D = 256
INNER = 128
FF = 2048
HEADS = 8
GRID = 64
QT = 7
BOXES = 8
STEP = 5
SLICES = 64
VOLS = 32
IMG = 4096
PARAMS_RAW = 1579008
PARAMS = 1579008


image_side_names = ('totok_q', 'totok_k', 'totok_v', 'totok_o', 'totok_bq', 'totok_bv', 'totok_bo', 'gain_4', 'shift_4')


def piece_table_drawn(width, inner, hidden):
    table = [('self_q', width, width, 'matrix', 1.0), ('self_k', width, width, 'matrix', 1.0), ('self_v', width, width, 'matrix', 1.0), ('self_o', width, width, 'matrix', 2.0), ('toimg_q', width, inner, 'matrix', 1.0), ('toimg_k', width, inner, 'matrix', 1.0), ('toimg_v', width, inner, 'matrix', 1.0), ('toimg_o', inner, width, 'matrix', 24.0), ('totok_q', width, inner, 'matrix', 1.0), ('totok_k', width, inner, 'matrix', 1.0), ('totok_v', width, inner, 'matrix', 1.0), ('totok_o', inner, width, 'matrix', 2.0), ('mlp_up', width, hidden, 'matrix', 1.0), ('mlp_down', hidden, width, 'matrix', 1.0), ('self_bq', 1, width, 'bias', 1.0), ('self_bv', 1, width, 'bias', 1.0), ('self_bo', 1, width, 'bias', 1.0), ('toimg_bq', 1, inner, 'bias', 1.0), ('toimg_bv', 1, inner, 'bias', 1.0), ('toimg_bo', 1, width, 'bias', 1.0), ('totok_bq', 1, inner, 'bias', 1.0), ('totok_bv', 1, inner, 'bias', 1.0), ('totok_bo', 1, width, 'bias', 1.0), ('mlp_bup', 1, hidden, 'bias', 1.0), ('mlp_bdown', 1, width, 'bias', 1.0)]
    for number in range(1, 5):
        table.append(('gain_' + str(number), 1, width, 'gain', 1.0))
    for number in range(1, 5):
        table.append(('shift_' + str(number), 1, width, 'bias', 1.0))
    return table


def piece_scale(name):
    base = 0.3 * math.sqrt(SLICES / 20.0)
    if name in image_side_names:
        return base * GRID
    return base * math.sqrt(QT)


def draw_box_mask(key, part):
    key = jax.random.fold_in(key, 5)
    first, second = jax.random.split(key)
    extra = jax.random.randint(first, (SLICES,), 0, 2)
    ranks = jnp.arange(SLICES, dtype=jnp.int32)
    live = jnp.minimum(2 + (BOXES - 2) * ranks // max(SLICES - 1, 1) + extra, BOXES)
    subkeys = jax.random.split(second, SLICES)
    order = jax.vmap(lambda sub: jax.random.permutation(sub, BOXES))(subkeys)
    return (order < live[:, None]).astype(jnp.int32)


def draw_master(key, part):
    key = jax.random.fold_in(key, 11)
    spread = 3.0
    pieces = []
    for index, entry in enumerate(piece_table_drawn(D, INNER, FF)):
        name, rows, cols, kind, boost = entry
        count = rows * cols
        first, second = jax.random.split(jax.random.fold_in(key, index))
        base = jax.random.truncated_normal(first, -4.0, 4.0, (count,), jnp.float32)
        position = (jnp.arange(count, dtype=jnp.float32) + 0.5) / count
        rising = jnp.exp(math.log(spread) * (position - 0.5))
        jitter = jnp.exp(jax.random.uniform(second, (count,), jnp.float32, -0.22, 0.22))
        if kind == 'matrix':
            pieces.append(base * rising * jitter * boost / math.sqrt(rows))
        elif kind == 'gain':
            pieces.append(rising * jitter)
        else:
            pieces.append(0.3 * base * jitter)
    pieces.append(0.1 * jax.random.normal(jax.random.fold_in(key, 999), (PARAMS - PARAMS_RAW,), jnp.float32))
    return jnp.concatenate(pieces)


def draw_moment1(key, part):
    key = jax.random.fold_in(key, 23)
    pieces = []
    for index, entry in enumerate(piece_table_drawn(D, INNER, FF)):
        count = entry[1] * entry[2]
        sub = jax.random.fold_in(key, index)
        base = jax.random.truncated_normal(sub, -3.0, 3.0, (count,), jnp.float32)
        pieces.append(base * piece_scale(entry[0]))
    pieces.append(0.01 * jax.random.normal(jax.random.fold_in(key, 999), (PARAMS - PARAMS_RAW,), jnp.float32))
    return jnp.concatenate(pieces)


def draw_moment2(key, part):
    key = jax.random.fold_in(key, 37)
    pieces = []
    for index, entry in enumerate(piece_table_drawn(D, INNER, FF)):
        count = entry[1] * entry[2]
        sub = jax.random.fold_in(key, index)
        factor = jnp.exp(jax.random.uniform(sub, (count,), jnp.float32, 0.0, math.log(4.0)))
        pieces.append(factor * piece_scale(entry[0]) ** 2)
    rest = jax.random.uniform(jax.random.fold_in(key, 999), (PARAMS - PARAMS_RAW,), jnp.float32, 0.5, 2.0)
    pieces.append(rest * 0.0001)
    return jnp.concatenate(pieces)


def plant(result, key, smallest, high):
    spot = [jax.random.randint(jax.random.fold_in(key, axis), (), 0, length) for axis, length in enumerate(result.shape)]
    longest = result.shape.index(max(result.shape))
    neighbour = spot[:longest] + [(spot[longest] + 1) % result.shape[longest]] + spot[longest + 1:]
    return result.at[tuple(spot)].set(smallest).at[tuple(neighbour)].set(high)


def block_scale(rng, dims, cuts, smallest, top_value):
    def one(dim, shards_of):
        draws = jax.random.uniform(jax.random.fold_in(jax.random.fold_in(rng, 6), dim), (shards_of,), jnp.float32, smallest / len(cuts), top_value / len(cuts))
        return jnp.repeat(jnp.exp(draws), dims[dim] // shards_of).reshape((-1,) + (1,) * (len(dims) - dim - 1))

    factor_of = one(*cuts[0])
    for cut in cuts[1:]:
        factor_of = factor_of * one(*cut)
    return factor_of


def profile(amount, total, most, skew):
    portions = [(1 << 20) // math.isqrt(grade ** skew) + 1 for grade in range(2, amount + 1)]
    spare, holding = total - most - (amount - 1), [1] * (amount - 1)
    while spare > 0:
        free = [i for i in range(amount - 1) if holding[i] < most]
        pool, budget = sum([portions[i] for i in free]), spare
        for i in free:
            addition = min(most - holding[i], max(1, budget * portions[i] // pool), spare)
            holding[i] = holding[i] + addition
            spare = spare - addition
    return np.array([most] + holding)


def ragged(own_key, count, total, limit, slope):
    if count == 2:
        one = jax.random.randint(own_key, (), max(1, total - limit), min(limit, total - 1) + 1)
        return jnp.stack([one, total - one])
    sizes = jnp.asarray(profile(count, total, limit, slope), jnp.int32)
    twos = (count - 1) // 2
    donor, receiver = sizes[1:1 + 2 * twos:2], sizes[2:2 + 2 * twos:2]
    slack = jnp.minimum(donor - 1, limit - receiver)
    shifted = jax.random.randint(jax.random.fold_in(own_key, 1), (twos,), 0, 1 << 20) % (slack + 1)
    sizes = sizes.at[1:1 + 2 * twos:2].set(donor - shifted).at[2:2 + 2 * twos:2].set(receiver + shifted)
    return sizes[jax.random.permutation(jax.random.fold_in(own_key, 2), count)]


def centred(stream_key, shape, scale, bound, cuts=(), kind=jnp.bfloat16):
    entries = scale * jax.random.normal(stream_key, shape, jnp.float32)
    if cuts:
        entries = entries * block_scale(stream_key, shape, cuts, -0.22, 0.18)
    return jnp.clip(entries, -bound, bound).astype(kind)


def setup_inputs(seed: int = 0) -> dict:
    splits = jax.random.split(jax.random.key(seed), 11)
    return {
        "queries_in": centred(splits[0], (SLICES, BOXES, QT, D), 1.0, 6.0, ((0, 64), (1, 2))),
        "image": centred(splits[1], (SLICES, IMG, D), 1.0, 6.0, ((0, 64), (1, 2))),
        "box_coords": plant(jax.random.randint(splits[2], (SLICES, BOXES, 4), 0, 1024), jax.random.fold_in(splits[2], 1), 0, 1023).astype(jnp.int32),
        "box_mask": draw_box_mask(jax.random.fold_in(splits[10], 71), 0),
        "volume_ids": jnp.searchsorted(jnp.cumsum(ragged(splits[4], VOLS, SLICES, 4, 0)), jnp.arange(SLICES), side="right").astype(jnp.int32),
        "cot_queries": centred(splits[5], (SLICES, BOXES, QT, D), 1.0, 6.0, ((0, 64), (1, 2))),
        "cot_keys": centred(splits[6], (SLICES, BOXES, IMG, D), 1.0, 6.0, ((0, 64), (1, 2))),
        "master": draw_master(jax.random.fold_in(splits[10], 71), 0),
        "moment1": draw_moment1(jax.random.fold_in(splits[10], 71), 0),
        "moment2": draw_moment2(jax.random.fold_in(splits[10], 71), 0),
    }


@jax.custom_vjp
def low(v):
    return lax.optimization_barrier(v.astype(jnp.bfloat16)).astype(jnp.float32)

@jax.custom_vjp
def low_back(v):
    return v

def low_keep(v):
    return (low(v), None)

def low_pass(kept, grad):
    return (grad,)

def back_keep(v):
    return (v, None)

def back_low(kept, grad):
    return (low(grad),)
low.defvjp(low_keep, low_pass)
low_back.defvjp(back_keep, back_low)

def piece_table(width, inner, hidden):
    table = [('self_q', width, width, 'matrix'), ('self_k', width, width, 'matrix'), ('self_v', width, width, 'matrix'), ('self_o', width, width, 'matrix'), ('toimg_q', width, inner, 'matrix'), ('toimg_k', width, inner, 'matrix'), ('toimg_v', width, inner, 'matrix'), ('toimg_o', inner, width, 'matrix'), ('totok_q', width, inner, 'matrix'), ('totok_k', width, inner, 'matrix'), ('totok_v', width, inner, 'matrix'), ('totok_o', inner, width, 'matrix'), ('mlp_up', width, hidden, 'matrix'), ('mlp_down', hidden, width, 'matrix'), ('self_bq', 1, width, 'bias'), ('self_bv', 1, width, 'bias'), ('self_bo', 1, width, 'bias'), ('toimg_bq', 1, inner, 'bias'), ('toimg_bv', 1, inner, 'bias'), ('toimg_bo', 1, width, 'bias'), ('totok_bq', 1, inner, 'bias'), ('totok_bv', 1, inner, 'bias'), ('totok_bo', 1, width, 'bias'), ('mlp_bup', 1, hidden, 'bias'), ('mlp_bdown', 1, width, 'bias')]
    for number in range(1, 5):
        table.append(('gain_' + str(number), 1, width, 'gain'))
    for number in range(1, 5):
        table.append(('shift_' + str(number), 1, width, 'bias'))
    return table

def unpack(flat, width, inner, hidden):
    found = {}
    offset = 0
    for name, rows, cols, kind in piece_table(width, inner, hidden):
        piece = flat[offset:offset + rows * cols]
        found[name] = piece.reshape(rows, cols) if kind == 'matrix' else piece
        offset += rows * cols
    return found

def segment_members(positions, width, inner, hidden):
    columns = []
    offset = 0
    for name, rows, cols, kind in piece_table(width, inner, hidden):
        if kind == 'matrix':
            columns.append((positions >= offset) & (positions < offset + rows * cols))
        offset += rows * cols
    return jnp.stack(columns, axis=1).astype(jnp.float32)

def product(left, right):
    return jnp.dot(left, right, precision=lax.Precision.HIGHEST, preferred_element_type=jnp.float32)

def fourier(across, down, width):
    order = jnp.arange(width // 2, dtype=jnp.float32)
    radius = 1.0 + jnp.mod(order, 4.0)
    turn = order * 2.39996
    phase = 2.0 * math.pi * (across[..., None] * radius * jnp.cos(turn) + down[..., None] * radius * jnp.sin(turn))
    return jnp.concatenate([jnp.sin(phase), jnp.cos(phase)], axis=-1)

def image_pe(grid, width):
    cells = jnp.arange(grid * grid, dtype=jnp.int32)
    across = 2.0 * ((cells % grid).astype(jnp.float32) + 0.5) / grid - 1.0
    down = 2.0 * ((cells // grid).astype(jnp.float32) + 0.5) / grid - 1.0
    return fourier(across, down, width)

def corner_pe(coords, tokens, width):
    points = (coords.astype(jnp.float32) + 0.5) / 1024.0 * 2.0 - 1.0
    first = fourier(points[..., 0], points[..., 1], width)
    second = fourier(points[..., 2], points[..., 3], width)
    blank = jnp.zeros(coords.shape[:-1] + (tokens - 2, width), jnp.float32)
    return jnp.concatenate([blank, first[..., None, :], second[..., None, :]], axis=-2)

def layer_norm(values, gain, shift):
    centered = values - lax.optimization_barrier(jnp.mean(values, axis=-1, keepdims=True))
    spread = lax.optimization_barrier(jnp.mean(centered * centered, axis=-1, keepdims=True))
    return centered * lax.rsqrt(spread + 1e-05) * gain + shift

def attend(source_q, source_k, source_v, w_query, b_query, w_key, w_value, b_value, w_out, b_out):
    query = product(source_q, w_query) + b_query
    keyed = product(source_k, w_key)
    valued = product(source_v, w_value) + b_value
    inner = query.shape[1]
    size = inner // HEADS
    query = query.reshape(query.shape[0], HEADS, size) / math.sqrt(size)
    keyed = keyed.reshape(keyed.shape[0], HEADS, size)
    valued = valued.reshape(valued.shape[0], HEADS, size)
    if query.shape[0] >= keyed.shape[0]:
        scores = jnp.einsum('khe,qhe->hkq', keyed, query, precision=lax.Precision.HIGHEST)
        probs = jax.nn.softmax(scores, axis=1)
        mixed = jnp.einsum('hkq,khe->qhe', probs, valued, precision=lax.Precision.HIGHEST)
    else:
        scores = jnp.einsum('qhe,khe->hqk', query, keyed, precision=lax.Precision.HIGHEST)
        probs = jax.nn.softmax(scores, axis=2)
        mixed = jnp.einsum('hqk,khe->qhe', probs, valued, precision=lax.Precision.HIGHEST)
    return product(mixed.reshape(mixed.shape[0], inner), w_out) + b_out

def block(flat, key_in, query_in, query_pe, key_pe):
    parts = unpack(flat, D, INNER, FF)
    mixed_in = query_in + query_pe
    branch = attend(mixed_in, mixed_in, query_in, parts['self_q'], parts['self_bq'], parts['self_k'], parts['self_v'], parts['self_bv'], parts['self_o'], parts['self_bo'])
    first = layer_norm(query_in + branch, parts['gain_1'], parts['shift_1'])
    located = key_in + key_pe
    branch = attend(first + query_pe, located, key_in, parts['toimg_q'], parts['toimg_bq'], parts['toimg_k'], parts['toimg_v'], parts['toimg_bv'], parts['toimg_o'], parts['toimg_bo'])
    second = layer_norm(first + branch, parts['gain_2'], parts['shift_2'])
    hidden = jax.nn.gelu(product(second, parts['mlp_up']) + parts['mlp_bup'], approximate=False)
    third = layer_norm(second + product(hidden, parts['mlp_down']) + parts['mlp_bdown'], parts['gain_3'], parts['shift_3'])
    branch = attend(located, third + query_pe, third, parts['totok_q'], parts['totok_bq'], parts['totok_k'], parts['totok_v'], parts['totok_bv'], parts['totok_o'], parts['totok_bo'])
    keys_out = layer_norm(key_in + branch, parts['gain_4'], parts['shift_4'])
    return (third, keys_out)

def reference(queries_in, image, box_coords, box_mask, volume_ids, cot_queries, cot_keys, master, moment1, moment2):
    belongs = (volume_ids[:, None] == jnp.arange(VOLS, dtype=jnp.int32)[None, :]).astype(jnp.float32)
    live = lax.optimization_barrier(jnp.sum(box_mask, axis=1)).astype(jnp.float32)
    counts = lax.optimization_barrier(jnp.sum(belongs * live[:, None], axis=0))
    per_slice = product(belongs, counts)
    scale = box_mask.astype(jnp.float32) / per_slice[:, None]
    key_pe = image_pe(GRID, D)
    query_pe = corner_pe(box_coords, QT, D)

    def one_slice(flat_grad, inputs):
        key_rows, queries, pe_rows, cot_q, cot_k, weight_row = inputs

        def forward(params, keys_value, query_value):
            flat = low(params)
            return jax.vmap(block, in_axes=(None, None, 0, 0, None))(flat, keys_value, query_value, pe_rows, key_pe)
        outputs, pullback = jax.vjp(forward, master, key_rows.astype(jnp.float32), queries.astype(jnp.float32))
        weight_col = weight_row[:, None, None]
        grads = pullback((cot_q.astype(jnp.float32) * weight_col, cot_k.astype(jnp.float32) * weight_col))
        return (flat_grad + grads[0], (outputs[0].astype(jnp.bfloat16), outputs[1].astype(jnp.bfloat16), grads[2], grads[1]))
    flat_grad, (queries_out, keys_out, queries_grad, image_grad) = lax.scan(one_slice, jnp.zeros(master.shape, jnp.float32), (image, queries_in, query_pe, cot_queries, cot_keys, scale))
    new_first = 0.5 * moment1 + 0.5 * flat_grad
    new_second = 0.5 * moment2 + 0.5 * flat_grad * flat_grad
    fix = 1.0 - 0.5 ** STEP
    update = new_first / fix / (jnp.sqrt(new_second / fix) + 1e-06) + 0.01 * master
    member = segment_members(jnp.arange(PARAMS, dtype=jnp.int32), D, INNER, FF)
    weight_norm = jnp.sqrt(product(master * master, member))
    update_norm = jnp.sqrt(product(update * update, member))
    ratio = weight_norm / (update_norm + 1e-06)
    entry_ratio = product(member, ratio) + (1.0 - lax.optimization_barrier(jnp.sum(member, axis=1)))
    new_master = master - 0.25 * entry_ratio * update
    matrix_norms = jnp.stack([weight_norm, update_norm])
    return (queries_out, keys_out, queries_grad, image_grad, new_master, new_first, new_second, new_master.astype(jnp.bfloat16), matrix_norms)
```

```python
import functools
import math

import jax
import jax.numpy as jnp
from jax import lax
from jax.experimental import pallas as pl
from jax.experimental.pallas import tpu as pltpu
from jax.sharding import Mesh
from jax.sharding import PartitionSpec as P

D = 256
INNER = 128
FF = 2048
HEADS = 8
GRID = 64
QT = 7
STEP = 5
CUTS = ("cuts_0", "cuts_1", "cuts_2", "cuts_3")
CUTS_BOX = ("cuts_0", "cuts_1", "cuts_2", "cuts_3", "box")
F32 = jnp.float32
BF = jnp.bfloat16
NEG = -1e30

MROWS = 12288
VLEN = 6144
VROWS = VLEN // 128
CHUNK = 112
PADDED = 12352
PEERS = 64
MATRIX_ROWS = (512, 512, 512, 512, 256, 256, 256, 256, 256, 256, 256, 256, 4096, 4096)
ROW0 = tuple(sum(MATRIX_ROWS[:i]) for i in range(15))
(SQ, SK, SV, SO, TQ, TK, TV, TO, UQ, UK, UV, UO, UP, DOWN) = ROW0[:14]
VECTORS = (
    ("s_bq", 256), ("s_bv", 256), ("s_bo", 256), ("t_bq", 128), ("t_bv", 128), ("t_bo", 256),
    ("u_bq", 128), ("u_bv", 128), ("u_bo", 256), ("bup", 2048), ("bdown", 256),
    ("g1", 256), ("g2", 256), ("g3", 256), ("g4", 256),
    ("h1", 256), ("h2", 256), ("h3", 256), ("h4", 256),
)
VOFF = {}
_at = 0
for _name, _len in VECTORS:
    VOFF[_name] = (_at, _len)
    _at += _len

TC = 512
IMG = GRID * GRID
STEPS = IMG // TC
HALF = STEPS // 2
TI = 1024
STEPS_I = IMG // TI
HALF_I = STEPS_I // 2
SENT = TC + 16 * (TC // 256)
RB = 64
SB = 64
PART0 = (0, 1, 2)
MIB = 1024 * 1024
MOST = 58 * MIB


def mm(a, b, ca=1, cb=0):
    return lax.dot_general(a, b, (((ca,), (cb,)), ((), ())), preferred_element_type=F32)


def split(x):
    hi = x.astype(BF)
    return hi, (x - hi.astype(F32)).astype(BF)


def mm_w(x, w, cb=0):
    hi, lo = split(x)
    rows = x.shape[0]
    y = mm(jnp.concatenate([hi, lo], axis=0), w, 1, cb)
    return y[:rows] + y[rows:]


def mm3(a, b, ca=1, cb=0):
    ah, al = split(a)
    bh, bl = split(b)
    return mm(ah, bh, ca, cb) + (mm(ah, bl, ca, cb) + mm(al, bh, ca, cb))


def mm3s(ah, al, bh, bl, ca=1, cb=0):
    return mm(ah, bh, ca, cb) + (mm(ah, bl, ca, cb) + mm(al, bh, ca, cb))


def cat3(a, dim):
    hi, lo = split(a)
    return jnp.concatenate([hi, hi, lo], axis=dim)


def cat3r(a, dim):
    hi, lo = split(a)
    return jnp.concatenate([hi, lo, hi], axis=dim)


def outer(a, b):
    ah, al = split(a)
    bh, bl = split(b)
    left = jnp.concatenate([ah, al, ah], axis=0)
    right = jnp.concatenate([bh, bh, bl], axis=0)
    return mm(left, right, 0, 0)


def iota(shape, dim):
    return lax.broadcasted_iota(jnp.int32, shape, dim)


def head_mask(width):
    c = iota((256, width), 0) % HEADS
    e = iota((256, width), 1) // (width // HEADS)
    return (c == e).astype(F32)


def expand(x, mask):
    n = x.shape[1]
    return jnp.broadcast_to(x[:, None, :], (32, HEADS, n)).reshape(256, n) * mask


def collapse(y, mask):
    n = y.shape[1]
    return jnp.sum((y * mask).reshape(32, HEADS, n), axis=1)


def live_rows(n):
    return (iota((32, n), 0) < 4 * QT).astype(F32)


def ln(x, gain, shift):
    centered = x - jnp.mean(x, axis=-1, keepdims=True)
    r = lax.rsqrt(jnp.mean(centered * centered, axis=-1, keepdims=True) + 1e-5)
    n = centered * r
    return n * gain + shift, n, r


def ln_back(dy, n, r, gain):
    h = dy * gain
    m1 = jnp.mean(h, axis=-1, keepdims=True)
    m2 = jnp.mean(h * n, axis=-1, keepdims=True)
    return r * (h - m1 - n * m2)


def col_sum(x):
    return jnp.sum(x, axis=0, keepdims=True)


def vget(ref, name):
    at, n = VOFF[name]
    row = at // 128
    return jnp.concatenate([ref[row + k : row + k + 1, :] for k in range(n // 128)], axis=1)


def wide(ref, row, n):
    left = ref[pl.ds(row, n, stride=2), :].astype(BF)
    right = ref[pl.ds(row + 1, n, stride=2), :].astype(BF)
    return jnp.concatenate([left, right], axis=1)


def pack256(ref, row, x):
    n = x.shape[0]
    ref[pl.ds(row, n, stride=2), :] = x[:, :128]
    ref[pl.ds(row + 1, n, stride=2), :] = x[:, 128:]


def chunk_row(p, core):
    device = (p // 2) * 4 + core * 2 + p % 2
    return pl.multiple_of(((771 * device) // 64) * 8, 8)


def fixed(x, dim=1):
    top = jnp.max(jnp.abs(x), axis=dim, keepdims=True)
    power = jnp.ceil(jnp.log2(jnp.maximum(top, 1e-30))) - 14.0
    return jnp.round(x * jnp.exp2(-power)).astype(jnp.int32), power


def on_lanes(column, rows):
    n = column.shape[0]
    return jnp.broadcast_to(column, (n, 128)).T[:rows]


def gelu_parts(x):
    cdf = 0.5 * (1.0 + lax.erf(x * math.sqrt(0.5)))
    return cdf


def in_vmem(n):
    return [pl.BlockSpec(memory_space=pltpu.VMEM)] * n


def specs(shapes):
    return [jax.ShapeDtypeStruct(shape, t) for shape, t, *_ in shapes]


def prep_kernel(half, sa, ca, sb, cb, *refs):
    k0_o, lh_o, ll_o, lht_o, llt_o, k0t_o = refs[-6:]
    k0 = half[...]
    rows = []
    for q in range(TC // GRID):
        s, c = sb[q : q + 1, :], cb[q : q + 1, :]
        rows.append(
            jnp.concatenate([sa[...] * c + ca[...] * s, ca[...] * c - sa[...] * s], axis=1)
        )
    loc = k0.astype(F32) + jnp.concatenate(rows, axis=0)
    hi, lo = split(loc)
    k0_o[...] = k0
    lh_o[...] = hi
    ll_o[...] = lo
    lht_o[...] = hi.T
    llt_o[...] = lo.T
    k0t_o[...] = k0.T


def prep(half, at, sa, ca, sb, cb, filled=()):
    col = pl.BlockSpec((D, TC), lambda j: (0, j + at))
    row = pl.BlockSpec((TC, D), lambda j: (j + at, 0))
    full = pl.BlockSpec((GRID, 128), lambda j: (0, 0))
    part = pl.BlockSpec((TC // GRID, 128), lambda j: (j + at, 0))
    rs = jax.ShapeDtypeStruct((IMG, D), BF)
    cs = jax.ShapeDtypeStruct((D, IMG), BF)
    return pl.pallas_call(
        prep_kernel,
        grid=(HALF,),
        in_specs=[pl.BlockSpec((TC, D), lambda j: (j, 0)), full, full, part, part]
        + [pl.BlockSpec(memory_space=pl.ANY)] * len(filled),
        out_specs=[row, row, row, col, col, col],
        out_shape=[rs, rs, rs, cs, cs, cs],
        input_output_aliases={5 + i: i for i in range(len(filled))},
        compiler_params=pltpu.CompilerParams(vmem_limit_bytes=MOST),
        cost_estimate=pl.CostEstimate(flops=10**9, bytes_accessed=8 * 10**6, transcendentals=0),
        name="prep",
    )(half, sa, ca, sb, cb, *filled)


HOPS = (0, -1, 1, 2)

STAT, SMALL, WT, TOK, TOK2, F1, U1, PRE, ROWS32 = 0, 16, 32, 64, 320, 448, 704, 960, 1216
NAR, NAR2, RR, VEC, PS, NARROW32 = 0, 32, 128, 224, 272, 528
SELF, TOW, UOW, UPB, DOWNB, ROWS16 = 0, 1024, 1152, 1280, 3328, 5376

G1, DM2, DF1, DPRE, DVW, DTOK, DNAR, DC2, DOTS, DGAIN, ROWSC = 0, 256, 512, 768, 1024, 1288, 1416, 1512, 1520, 1528, 1560


def tok32(ref, row, k):
    return ref[row + 32 * k : row + 32 * k + 32, :]


def up_blocks(w):
    return [w[UPB + 256 * k : UPB + 256 * k + 256, :] for k in range(8)]


def lay_weights(place, pieces, w_s, notes_s):
    core, y0 = place[1], place[2]
    w_s[...] = jnp.zeros((PADDED, 128), F32)
    keep = (iota((8, 128), 0) < 7).astype(F32)
    for at, n, copies, refs in pieces:
        for copy in copies:
            copy.wait()

        def lay(p, carry, refs=refs):
            k = p % 4
            y = (y0 + jnp.where(k == 1, 3, jnp.where(k == 2, 1, jnp.where(k == 3, 2, 0)))) % 4
            for ref, c, seen in zip(refs, (core, 1 - core), (0, PEERS)):
                device = (p // 16) * 32 + (y // 2) * 16 + ((p // 4) % 4) * 4 + c * 2 + y % 2
                row = ((771 * device) // 64) * 8
                block = ref[p].astype(F32)
                for lo, hi in ((0, 16), (16, 96), (96, CHUNK - 8), (CHUNK - 8, CHUNK)):
                    to = pl.ds(pl.multiple_of(row + lo, 8), hi - lo)
                    part = block[lo:hi]
                    if hi == CHUNK:
                        part = part * keep
                    w_s[to, :] = part if lo == 16 else w_s[to, :] + part
                notes_s[pl.ds(seen + p, 1), :] = block[CHUNK - 1 :, :]
            return carry

        lax.fori_loop(at, at + n, lay, 0, unroll=2)


def tokens_kernel(
    place, q0_i, pe_i, mine_h, other_h, lh_h, ll_h, k0t_h,
    s1_h, big_h, a32_h, b32_h, w16_h, slim_h,
    s1_o, big, a32, b32, w16, slim,
    w_s, notes_s, ut, mine_i, other_i, lh_i, ll_i, k0t_i, sems, sems_out,
):
    vec = b32.at[VEC : VEC + VROWS]
    leaving = []

    def leave(k, src, dst):
        copy = pltpu.make_async_copy(src, dst, sems_out.at[k])
        copy.start()
        leaving.append(copy)

    quarter = PEERS // 4
    pieces = []
    for k in range(4):
        part = pl.ds(k * quarter, quarter)
        copies = [
            pltpu.make_async_copy(src.at[part], dst.at[part], sems.at[2 * k + n])
            for n, (src, dst) in enumerate(((mine_h, mine_i), (other_h, other_i)))
        ]
        for copy in copies:
            copy.start()
        pieces.append((k * quarter, quarter, copies, (mine_i, other_i)))
    later = [
        pltpu.make_async_copy(src, dst, sems.at[8 + n])
        for n, (src, dst) in enumerate(((lh_h, lh_i), (ll_h, ll_i), (k0t_h, k0t_i)))
    ]
    for copy in later:
        copy.start()
    lay_weights(place, pieces, w_s, notes_s)
    notes = notes_s[...]
    same = notes[:, 4:5] == place[3].astype(F32)
    lane128 = iota((128, 128), 1)
    count = jnp.sum(col_sum(jnp.where(same & (lane128 < 4), notes, 0.0)), axis=1, keepdims=True)
    weights = [place[4 + b].astype(F32) / count for b in range(4)]
    a32[0:TOK, :] = jnp.zeros((TOK, 256), F32)
    for b in range(4):
        a32[WT + b : WT + b + 1, :] = jnp.broadcast_to(weights[b], (1, 256))
    vec[...] = w_s[MROWS : MROWS + VROWS, :]
    for k, at in enumerate((TQ, TK, TV, UQ, UK, UV)):
        slim[k] = w_s[at : at + 256, :].astype(BF)
    leave(0, slim, slim_h)
    for k, at in enumerate((SQ, SK, SV, SO)):
        w16[SELF + 256 * k : SELF + 256 * k + 256, :] = wide(w_s, at, 256)
    w16[TOW : TOW + 128, :] = wide(w_s, TO, 128)
    w16[UOW : UOW + 128, :] = wide(w_s, UO, 128)

    def self_w(k):
        return w16[SELF + 256 * k : SELF + 256 * k + 256, :]

    q0 = q0_i[...]
    pe = pe_i[...]
    m = q0 + pe
    q = mm_w(m, self_w(0)) + vget(vec, "s_bq")
    k = mm_w(m, self_w(1))
    v = mm_w(q0, self_w(2)) + vget(vec, "s_bv")
    m256 = head_mask(D)
    m128 = head_mask(INNER)
    qe = expand(q * (1.0 / math.sqrt(D // HEADS)), m256)
    s = mm3(qe, k, 1, 1)
    c = iota((256, 32), 0)
    r = iota((256, 32), 1)
    valid = ((c // HEADS) % 4 == r % 4) & (r < 4 * QT)
    s = jnp.where(valid, s, NEG)
    e = jnp.exp(s - jnp.max(s, axis=1, keepdims=True))
    p = e / jnp.sum(e, axis=1, keepdims=True)
    o = collapse(mm3(p, v), m256)
    a = mm_w(o, self_w(3)) + vget(vec, "s_bo")
    q1, n1, r1 = ln(q0 + a, vget(vec, "g1"), vget(vec, "h1"))
    qt = mm_w(q1 + pe, slim[0]) + vget(vec, "t_bq")
    qx = expand(qt * (1.0 / math.sqrt(INNER // HEADS)), m128)
    f1 = mm_w(qx, slim[1], 1)
    for at, x in enumerate((m, q0, q, k, v, o, n1, q1)):
        a32[TOK + 32 * at : TOK + 32 * at + 32, :] = x
    b32[NAR : NAR + 32, :] = qt
    b32[RR : RR + 32, :] = jnp.broadcast_to(r1, (32, 128))
    b32[PS : PS + 256, :] = jnp.concatenate([p, jnp.zeros((256, 96), F32)], axis=1)
    a32[F1 : F1 + 256, :] = f1
    f1t = cat3r(f1.T, 0)
    for copy in later:
        copy.wait()
    top = jnp.full((1, 256), NEG, F32)
    for j in range(STEPS_I):
        at = slice(j * TI, j * TI + TI)
        lh = lh_i[at, :]
        s1 = mm(jnp.concatenate([lh, lh, ll_i[at, :]], axis=1), f1t)
        s1_o[at, :] = s1
        top = jnp.maximum(top, jnp.max(s1, axis=0, keepdims=True))
    leave(1, s1_o, s1_h)
    total = jnp.zeros((1, 256), F32)
    for j in range(STEPS_I):
        at = slice(j * TI, j * TI + TI)
        e = jnp.exp(s1_o[at, :] - top)
        total = total + col_sum(e)
        eh, el = split(e)
        k0t = k0t_i[:, at]
        part = mm(jnp.concatenate([k0t, k0t], axis=1), jnp.concatenate([eh, el], axis=0))
        ut[...] = part if j == 0 else ut[...] + part
    for k in range(16):
        at = UPB + 256 * (k // 2)
        lanes = slice(128 * (k % 2), 128 * (k % 2) + 128)
        w16[at : at + 256, lanes] = w_s[pl.ds(UP + k, 256, stride=16), :].astype(BF)
    for k in range(8):
        w16[DOWNB + 256 * k : DOWNB + 256 * k + 256, :] = wide(w_s, DOWN + 512 * k, 256)
    leave(2, w16, w16_h)
    inverse = 1.0 / total
    a32[STAT : STAT + 1, :] = top
    a32[STAT + 1 : STAT + 2, :] = inverse
    u1 = (ut[...] * inverse).T
    a32[U1 : U1 + 256, :] = u1
    mixed = collapse(mm_w(u1, slim[2]), m128) + vget(vec, "t_bv")
    a = mm_w(mixed, w16[TOW : TOW + 128, :]) + vget(vec, "t_bo")
    q2, n2, r2 = ln(q1 + a, vget(vec, "g2"), vget(vec, "h2"))
    pre = jnp.concatenate([mm_w(q2, w) for w in up_blocks(w16)], axis=1) + vget(vec, "bup")
    for k in range(8):
        a32[PRE + 32 * k : PRE + 32 * k + 32, :] = pre[:, 256 * k : 256 * k + 256]
    hid = pre * gelu_parts(pre)
    y = mm_w(hid, w16[DOWNB : DOWNB + FF, :]) + vget(vec, "bdown")
    q3, n3, r3 = ln(q2 + y, vget(vec, "g3"), vget(vec, "h3"))
    live = live_rows(INNER)
    k2 = mm_w(q3 + pe, slim[4]) * live
    v2 = (mm_w(q3, slim[5]) + vget(vec, "u_bv")) * live
    for at, x in enumerate((n2, q2, n3, q3)):
        a32[TOK2 + 32 * at : TOK2 + 32 * at + 32, :] = x
    leave(6, a32.at[TOK:ROWS32], a32_h.at[TOK:ROWS32])
    for at, x in enumerate((mixed, k2, v2)):
        b32[NAR2 + 32 * at : NAR2 + 32 * at + 32, :] = x
    b32[RR + 32 : RR + 64, :] = jnp.broadcast_to(r2, (32, 128))
    b32[RR + 64 : RR + 96, :] = jnp.broadcast_to(r3, (32, 128))
    leave(3, b32, b32_h)
    kx = expand(k2 * (1.0 / math.sqrt(INNER // HEADS)), m128)
    m2 = mm_w(kx, slim[3], 1)
    c2 = mm3(jnp.broadcast_to(vget(vec, "u_bq"), (8, INNER)), kx, 1, 1)[0:1, :]
    lane = iota((1, 256), 1)
    a32[SMALL : SMALL + 8, :] = jnp.broadcast_to(jnp.where(lane >= 224, NEG, c2), (8, 256))
    rows = iota((256, 1), 0)
    spare = (rows >= 224) & (rows % 8 == 0)
    big[0:768, :] = cat3r(jnp.where(spare, -1.0, m2), 0)
    big[768:1536, :] = cat3r(m2.T, 0)
    leave(7, big.at[0:BIG_W], big_h.at[0:BIG_W])
    vw = mm_w(expand(v2, m128), w16[UOW : UOW + 128, :])
    wc = vw - jnp.mean(vw, axis=1, keepdims=True)
    bo = vget(vec, "u_bo")
    bo = bo - jnp.mean(bo, axis=1, keepdims=True)
    wfull = jnp.where(spare, bo, wc)
    wh = wfull.astype(BF).astype(F32)
    wl = wfull - wh
    rolled = jnp.concatenate([wh[248:], wh[:248]], axis=0)
    low = jnp.concatenate([wl[240:], wl[:240]], axis=0)
    cls = (rows // 8) % 4
    wt = wc.T
    lane_cls = (lane // 8) % 4
    wth = wt.astype(BF).astype(F32)
    wtl = pltpu.roll(wt - wth, 8, 1)
    gain = vget(vec, "g4")
    gain_col = jnp.broadcast_to(gain, (8, 256)).T[:, 0:1]
    row_o = a32.at[SMALL + 8 : SMALL + 16]
    for b in range(4):
        ws = jnp.where(
            cls == b, wh, jnp.where(cls == (b + 1) % 4, rolled, jnp.where(cls == (b + 2) % 4, low, 0.0))
        )
        big[BIG_W + 256 * b : BIG_W + 256 * b + 256, :] = ws.astype(BF)
        scaled = gain_col * weights[b]
        a = jnp.where(lane == 224 + 8 * b, scaled * (1.0 / D), wt * scaled)
        ah = a.astype(BF).astype(F32)
        al = pltpu.roll(a - ah, 8, 1)
        at = BIG_A + 1024 * (b % 2) + 512 * (b // 2)
        big[at : at + 256, :] = jnp.where(
            lane_cls == b, ah, jnp.where(lane_cls == (b + 1) % 4, al, 0.0)
        ).astype(BF)
        big[at + 256 : at + 512, :] = jnp.where(
            lane_cls == b, -wth, jnp.where(lane_cls == (b + 1) % 4, -wtl, 0.0)
        ).astype(BF)
        row_o[b : b + 1, :] = gain * weights[b]
    row_o[4:5, :] = gain
    row_o[5:6, :] = vget(vec, "h4")
    leave(4, big.at[BIG_W:BIG], big_h.at[BIG_W:BIG])
    leave(5, a32.at[0:TOK], a32_h.at[0:TOK])
    for copy in leaving:
        copy.wait()


BIG_W = 1536
BIG_A = BIG_W + 1024
BIG = BIG_A + 2048


def tokens(place, q0, pe, mine, other, lh, ll, k0t):
    out = [
        ((IMG, 256), F32),
        ((BIG, 256), BF),
        ((ROWS32, 256), F32),
        ((NARROW32, 128), F32),
        ((ROWS16, 256), BF),
        ((6, 256, 128), BF),
    ]
    return pl.pallas_call(
        tokens_kernel,
        in_specs=[pl.BlockSpec(memory_space=pltpu.SMEM)]
        + in_vmem(2)
        + [pl.BlockSpec(memory_space=pl.ANY)] * 5,
        out_specs=[pl.BlockSpec(memory_space=pl.ANY)] * len(out),
        out_shape=specs(out),
        scratch_shapes=[pltpu.VMEM(shape, t) for shape, t in out]
        + [
            pltpu.VMEM((PADDED, 128), F32),
            pltpu.VMEM((2 * PEERS, 128), F32),
            pltpu.VMEM((256, 256), F32),
            pltpu.VMEM((PEERS, CHUNK, 128), BF),
            pltpu.VMEM((PEERS, CHUNK, 128), BF),
            pltpu.VMEM((IMG, D), BF),
            pltpu.VMEM((IMG, D), BF),
            pltpu.VMEM((D, IMG), BF),
            pltpu.SemaphoreType.DMA((11,)),
            pltpu.SemaphoreType.DMA((len(out) + 2,)),
        ],
        compiler_params=pltpu.CompilerParams(vmem_limit_bytes=MOST),
        cost_estimate=pl.CostEstimate(flops=2 * 10**10, bytes_accessed=3 * 10**7, transcendentals=0),
        name="tokens",
    )(place, q0, pe, mine, other, lh, ll, k0t)


def group_max(x):
    m = jnp.maximum(x[:, :128], x[:, 128:])
    m = jnp.maximum(m, pltpu.roll(m, 64, 1))
    return jnp.maximum(m, pltpu.roll(m, 32, 1))


def group_sum(x):
    m = x[:, :128] + x[:, 128:]
    m = m + pltpu.roll(m, 64, 1)
    return m + pltpu.roll(m, 32, 1)


def twice(m):
    return jnp.concatenate([m, m], axis=1)


def image_kernel(
    place, cot_i, k0_i, lh_i, ll_i, lht_i, llt_i, s1_i, big_i, small_i, cq_i, *refs,
):
    late_refs, held, sems = refs[:4], refs[-5:-1], refs[-1]
    a32, b32, w16, slim = held
    later = [pltpu.make_async_copy(src, dst, sems.at[k]) for k, (src, dst) in enumerate(zip(late_refs, held))]
    image_steps(
        place, cot_i, k0_i, lh_i, ll_i, lht_i, llt_i, s1_i, big_i, small_i, cq_i, a32, b32, w16, slim, later, *refs[4:-5]
    )


def image_steps(
    place, cot_i, k0_i, lh_i, ll_i, lht_i, llt_i, s1_i, big_i, small_i, cq_i, a32, b32, w16, slim, later,
    keys_o, img_o, part0_o, part1_o, part2_o, c32,
    s_s, p_s, left_s, b_s, n_s, r_s, x_s, kc_s, acc, g2_o, dut, both,
):
    j = pl.program_id(0)

    @pl.when(j == 0)
    def _():
        for copy in later:
            copy.start()
        c32[...] = jnp.zeros((ROWSC, 256), F32)
        g2_o[...] = jnp.zeros(g2_o.shape, F32)

    @pl.when(j < STEPS_I)
    def _():
        image_part(
            cot_i, k0_i, lh_i, ll_i, lht_i, llt_i, big_i, small_i, keys_o,
            acc.at[pl.ds(pl.multiple_of(j * TI, TI), TI)], c32, g2_o,
            s_s, p_s, left_s, b_s, n_s, r_s, x_s, kc_s,
        )

    @pl.when(j == STEPS_I)
    def _():
        for copy in later:
            copy.wait()
        chain_part(cq_i, a32, b32, w16, slim, c32, g2_o, dut, both)

    def step(at, keep):
        image_step(
            s1_i, k0_i, lht_i, llt_i, acc.at[at * TI : at * TI + TI], a32, dut, both,
            c32.at[DOTS : DOTS + 8], c32.at[DF1 : DF1 + 256], keep,
        )

    def keep_send(refs, n, img):
        send(refs[n], img)

    def keep_own(n, img):
        img_o[n * TC : n * TC + TC, :] = img

    for n, refs in enumerate(((part0_o, part1_o), (part2_o.at[0:SENT], part2_o.at[SENT:]))):
        pl.when(j == STEPS_I + n)(functools.partial(step, HALF_I + n, functools.partial(keep_send, refs)))
    for n in range(HALF_I):
        pl.when(j == STEPS_I + HALF_I + n)(functools.partial(step, n, keep_own))


def image_part(
    cot_i, k0_i, lh_i, ll_i, lht_i, llt_i, big_i, small_i, keys_o, acc_o, c32, g2_o,
    s_s, p_s, left_s, b_s, n_s, r_s, x_s, kc_s,
):
    lh = lh_i[...]
    s_s[...] = mm(jnp.concatenate([lh, lh, ll_i[...]], axis=1), big_i[768:1536, :])
    lane = iota((SB, 256), 1)
    cls = (lane // 8) % 4
    for i in range(TI // SB):
        at = slice(i * SB, i * SB + SB)
        kf = k0_i[at, :].astype(F32)
        kc_s[at, :] = kf - jnp.mean(kf, axis=1, keepdims=True)
        s = s_s[at, :] + small_i[0:1, :]
        e = jnp.exp(s - twice(group_max(s)))
        p = e * twice(1.0 / group_sum(e))
        p = jnp.where((lane >= 224) & (lane % 8 == 0), 1.0, p)
        p_s[at, :] = p
        ph = p.astype(BF).astype(F32)
        plow = pltpu.roll(p - ph, 8, 1)
        pr = pltpu.roll(ph, 16, 1)
        for b in range(4):
            x = jnp.where(cls == b, ph, jnp.where(cls == (b + 1) % 4, plow, pr))
            left_s[b, at, :] = x.astype(BF)

    def product(b):
        b_s[b] = mm(left_s[b], big_i[BIG_W + 256 * b : BIG_W + 256 * b + 256, :])

    def box(b):
        for i in range(TI // RB):
            at = slice(i * RB, i * RB + RB)
            z = kc_s[at, :] + b_s[b, at, :]
            r = lax.rsqrt(jnp.mean(z * z, axis=1, keepdims=True) + 1e-5)
            n = z * r
            keys_o[b, at, :] = (n * small_i[12:13, :] + small_i[13:14, :]).astype(BF)
            g = cot_i[b, at, :].astype(F32)
            gn = g * n
            c32[DGAIN + 8 * b : DGAIN + 8 * b + 8, :] += jnp.sum(gn.reshape(RB // 8, 8, 256), axis=0)
            gain = small_i[8 + b : 9 + b, :]
            m2 = jnp.mean(gn * gain, axis=1, keepdims=True)
            nm = n * m2
            n_s[b, at, :] = nm.astype(BF)
            dz = r * (g * gain - nm)
            if b == 0:
                acc_o[at, :] = dz
            else:
                acc_o[at, :] += dz
            r_s[b, at, :] = jnp.broadcast_to(r, (RB, 128))

    def back_product(b):
        x_s[b] = mm(
            jnp.concatenate([cot_i[b], n_s[b], cot_i[b + 2], n_s[b + 2]], axis=1),
            big_i[BIG_A + 1024 * b : BIG_A + 1024 * b + 1024, :],
        )

    product(0)
    product(2)
    box(0)
    product(1)
    box(2)
    product(3)
    back_product(0)
    box(1)
    box(3)
    back_product(1)

    half = iota((SB, 128), 1)
    kind = (half // 8) % 4
    even = (lane // 8) % 2 == 0
    for i in range(TI // SB):
        at = slice(i * SB, i * SB + SB)
        rr = jnp.where(
            kind == 0,
            r_s[0, at, :],
            jnp.where(kind == 1, r_s[1, at, :], jnp.where(kind == 2, r_s[2, at, :], r_s[3, at, :])),
        )
        rr = twice(rr)
        xe = x_s[0, at, :]
        xo = x_s[1, at, :]
        x = jnp.where(even, xe, xo) + pltpu.roll(jnp.where(even, xo, xe), 248, 1)
        p = p_s[at, :]
        t = jnp.where(lane < 224, p, 0.0)
        dp = rr * x
        tdp = t * dp
        ds = tdp - t * twice(group_sum(tdp))
        s_s[at, :] = jnp.where((lane >= 224) & (lane % 8 == 0), dp, ds)
        p_s[at, :] = jnp.where((lane >= 224) & (lane % 8 == 1), 1.0, p * rr)

    ds = s_s[...]
    dh, dl = split(ds)
    acc_o[...] += mm(jnp.concatenate([dh, dh, dl], axis=1), big_i[0:768, :])
    lht = lht_i[...]
    c32[DM2 : DM2 + 256, :] += mm(
        jnp.concatenate([lht, llt_i[...], lht], axis=1), jnp.concatenate([dh, dh, dl], axis=0)
    )
    c32[DC2 : DC2 + 1, :] += col_sum(ds)
    l1 = p_s[...].T
    for b in range(4):
        pick = [l1[32 * i + 8 * b : 32 * i + 8 * b + 8] for i in range(8)]
        hi, lo = split(jnp.concatenate(pick, axis=0))
        y = mm(jnp.concatenate([hi, lo], axis=0), cot_i[b])
        c32[G1 + 64 * b : G1 + 64 * b + 64, :] += y[:64] + y[64:]
        g2_o[b] += mm(hi, n_s[b])


def image_side(place, cot, k0, lh, ll, lht, llt, s1, big, cq, a32, b32, w16, slim):
    def const(*shape):
        return pl.BlockSpec(shape, lambda j, place: (0,) * len(shape))

    def once(*shape):
        return pl.BlockSpec(shape, lambda j, place: (0,) * len(shape), pipeline_mode=pl.Buffered(1))

    def now(j):
        return jnp.minimum(j, STEPS_I - 1)

    def again(j):
        return jnp.where(j < STEPS_I, j, lax.rem(j + HALF_I, STEPS_I))

    row = pl.BlockSpec((TI, D), lambda j, place: (now(j), 0))
    row2 = pl.BlockSpec((TI, D), lambda j, place: (again(j), 0))
    col2 = pl.BlockSpec((D, TI), lambda j, place: (0, again(j)))
    late = pl.BlockSpec((TI, D), lambda j, place: (jnp.where(j < STEPS_I, HALF_I, again(j)), 0))
    boxes = pl.BlockSpec((4, TI, D), lambda j, place: (0, lax.rem(now(j) + place[0] * HALF_I, STEPS_I), 0))
    own = pl.BlockSpec((TI, D), lambda j, place: (jnp.maximum(j - STEPS_I - HALF_I, 0), 0))
    out = [
        ((4, IMG, D), BF, boxes),
        ((IMG // 2, D), F32, own),
        ((SENT, D), jnp.int16, None),
        ((SENT, D), jnp.int16, None),
        ((2 * SENT, D), jnp.int16, None),
        ((ROWSC, 256), F32, None),
    ]
    whole = [a32, b32, w16, slim]
    return pl.pallas_call(
        image_kernel,
        grid_spec=pltpu.PrefetchScalarGridSpec(
            num_scalar_prefetch=1,
            grid=(2 * STEPS_I,),
            in_specs=[boxes, row2, row, row, col2, col2, late, once(*big.shape)]
            + [pl.BlockSpec((16, 256), lambda j, place: (SMALL // 16, 0)), once(*cq.shape)]
            + [pl.BlockSpec(memory_space=pl.ANY)] * len(whole),
            out_specs=[s if s is not None else const(*shape) for shape, _, s in out],
            scratch_shapes=[
                pltpu.VMEM((TI, 256), F32),
                pltpu.VMEM((TI, 256), F32),
                pltpu.VMEM((4, TI, 256), BF),
                pltpu.VMEM((4, TI, 256), F32),
                pltpu.VMEM((4, TI, 256), BF),
                pltpu.VMEM((4, TI, 128), F32),
                pltpu.VMEM((2, TI, 256), F32),
                pltpu.VMEM((TI, 256), F32),
                pltpu.VMEM((IMG, 256), F32),
                pltpu.VMEM((4, 64, 256), F32),
                pltpu.VMEM((512, 256), BF),
                pltpu.VMEM((1536, 256), BF),
            ]
            + [pltpu.VMEM(x.shape, x.dtype) for x in whole]
            + [pltpu.SemaphoreType.DMA((len(whole),))],
        ),
        out_shape=specs(out),
        compiler_params=pltpu.CompilerParams(vmem_limit_bytes=MOST),
        cost_estimate=pl.CostEstimate(flops=5 * 10**10, bytes_accessed=4 * 10**7, transcendentals=0),
        name="image_side",
    )(place, cot, k0, lh, ll, lht, llt, s1, big, a32, cq, *whole)


def image_step(s1_i, k0_i, lht_i, llt_i, acc_i, stat_i, dut, both, dots, df1, keep):
    for n in range(TI // TC):
        at = slice(n * TC, n * TC + TC)
        k0 = k0_i[at, :]
        p = jnp.exp(s1_i[at, :] - stat_i[0:1, :]) * stat_i[1:2, :]
        dp = mm(jnp.concatenate([k0, k0], axis=1), dut[...])
        ds = p * (dp - dots[0:1, :])
        ph, plow = split(p)
        dh, dl = split(ds)
        img = acc_i[at, :] + mm(jnp.concatenate([ph, ph, plow, dh, dh, dl], axis=1), both[...])
        lht = lht_i[:, at]
        df1[...] += mm(
            jnp.concatenate([lht, llt_i[:, at], lht], axis=1), jnp.concatenate([dh, dh, dl], axis=0)
        )
        keep(n, img)


def send(ref, img):
    q, k = fixed(img)
    ref[0:TC, :] = q.astype(jnp.int16)
    k = on_lanes(k, 16).astype(jnp.int32).astype(jnp.int16)
    for part in range(TC // D):
        ref[TC + 16 * part : TC + 16 * part + 16, :] = k[:, D * part : D * part + D]


def chain_part(cq_i, a32, b32, w16, slim, c32, g2_i, dut, both):
    m128 = head_mask(INNER)
    scale1 = 1.0 / math.sqrt(INNER // HEADS)
    vec = b32.at[VEC : VEC + VROWS]
    per_box = []
    for b in range(4):
        gain = a32[SMALL + 8 + b : SMALL + 9 + b, :]
        x = c32[G1 + 64 * b : G1 + 64 * b + 64, :] * gain - g2_i[b]
        per_box.append(x - jnp.mean(x, axis=1, keepdims=True))
    bo_sum = sum(x[56:57] for x in per_box)
    zero = jnp.zeros((8, 256), F32)
    dvw = jnp.concatenate(
        [per_box[b][8 * i : 8 * i + 8] if i < QT else zero for i in range(8) for b in range(4)],
        axis=0,
    )
    c32[DVW : DVW + 256, :] = dvw
    c32[DVW + 256 : DVW + 264, :] = jnp.broadcast_to(bo_sum, (8, 256))
    dv2 = collapse(mm_w(dvw, w16[UOW : UOW + 128, :], 1), m128)
    dc2_8 = jnp.broadcast_to(c32[DC2 : DC2 + 1, :], (8, 256))
    dk2x = mm_w(c32[DM2 : DM2 + 256, :].T, slim[3]) + dc2_8.T[:, 0:1] * vget(vec, "u_bq")
    dk2 = collapse(dk2x, m128) * scale1 * live_rows(INNER)
    box = iota((32, 1), 0) % 4
    weight = sum(jnp.where(box == b, a32[WT + b : WT + b + 1, 0:1], 0.0) for b in range(4))
    dq3 = cq_i[...] * weight + mm_w(dv2, slim[5], 1) + mm_w(dk2, slim[4], 1)
    dx3 = ln_back(dq3, tok32(a32, TOK2, 2), b32[RR + 64 : RR + 96, 0:1], vget(vec, "g3"))
    pre = jnp.concatenate([tok32(a32, PRE, k) for k in range(8)], axis=1)
    slope = gelu_parts(pre) + pre * (jnp.exp(-0.5 * pre * pre) * (1.0 / math.sqrt(2.0 * math.pi)))
    dpre = mm_w(dx3, w16[DOWNB : DOWNB + FF, :], 1) * slope
    dq2 = dx3 + sum(
        mm_w(dpre[:, 256 * k : 256 * k + 256], w, 1) for k, w in enumerate(up_blocks(w16))
    )
    dx2 = ln_back(dq2, tok32(a32, TOK2, 0), b32[RR + 32 : RR + 64, 0:1], vget(vec, "g2"))
    dmixed = mm_w(dx2, w16[TOW : TOW + 128, :], 1)
    du = mm_w(expand(dmixed, m128), slim[2], 1)
    dots = jnp.sum(du * a32[U1 : U1 + 256, :], axis=1, keepdims=True)
    c32[DOTS : DOTS + 8, :] = jnp.broadcast_to(dots, (256, 128)).T[0:8, :]
    duh, dul = split(du.T)
    dut[...] = jnp.concatenate([duh, dul], axis=0)
    both[...] = jnp.concatenate([cat3r(du, 0), cat3r(a32[F1 : F1 + 256, :], 0)], axis=0)
    for at, x in enumerate((dv2, dk2, dmixed)):
        c32[DNAR + 32 * at : DNAR + 32 * at + 32, 0:128] = x
    for at, x in enumerate((dq3, dx3, dq2, dx2)):
        c32[DTOK + 32 * at : DTOK + 32 * at + 32, :] = x
    for k in range(8):
        c32[DPRE + 32 * k : DPRE + 32 * k + 32, :] = dpre[:, 256 * k : 256 * k + 256]


def land_kernel(img, part, out):
    k = jnp.concatenate([part[TC + 16 * i : TC + 16 * i + 1, :] for i in range(TC // D)], axis=1)
    scale = jnp.exp2(jnp.broadcast_to(k.astype(F32), (8, TC)).T[:, 0:1])
    out[...] = img[...] + part[0:TC, :].astype(F32) * scale


def land(img, part, at):
    row = pl.BlockSpec((TC, D), lambda j: (j + at, 0))
    return pl.pallas_call(
        land_kernel,
        grid=(part.shape[0] // SENT,),
        in_specs=[row, pl.BlockSpec((SENT, D), lambda j: (j, 0))],
        out_specs=row,
        out_shape=jax.ShapeDtypeStruct(img.shape, F32),
        input_output_aliases={0: 0},
        compiler_params=pltpu.CompilerParams(vmem_limit_bytes=6 * MIB),
        name="land",
    )(img, part)


def vputter(ref, row0):
    def vput(name, x):
        at, n = VOFF[name]
        for k in range(n // 128):
            row = MROWS - row0 + at // 128 + k
            ref[row : row + 1, :] = x[:, 128 * k : 128 * k + 128]

    return vput


def grads_kernel(
    place, pe_i, a32, b32, slim, c32, w16_h,
    mine_o, other_o, dq_o,
    gm_o, self_i, sem,
):
    weights = pltpu.make_async_copy(w16_h.at[SELF : SELF + 1024], self_i, sem)
    weights.start()
    vec = b32.at[VEC : VEC + VROWS]
    m128 = head_mask(INNER)
    scale1 = 1.0 / math.sqrt(INNER // HEADS)
    vput = vputter(gm_o, 0)
    gm_o[MROWS:, :] = jnp.zeros((PADDED - MROWS, 128), F32)
    pe = pe_i[...]
    dv2, dk2, dmixed = (tok32(c32, DNAR, k)[:, 0:128] for k in range(3))
    dq3, dx3, dq2, dx2 = (tok32(c32, DTOK, k) for k in range(4))
    n2, q2, n3, q3 = (tok32(a32, TOK2, k) for k in range(4))
    mixed, k2, v2 = (tok32(b32, NAR2, k) for k in range(3))
    vput("g3", col_sum(dq3 * n3))
    vput("h3", col_sum(dq3))
    vput("bdown", col_sum(dx3))
    for g in range(8):
        pre = tok32(a32, PRE, g)
        pack256(gm_o, DOWN + 512 * g, outer(pre * gelu_parts(pre), dx3))
    dpre = [tok32(c32, DPRE, g) for g in range(8)]
    vput("bup", col_sum(jnp.concatenate(dpre, axis=1)))
    for g in range(8):
        y = outer(q2, dpre[g])
        gm_o[pl.ds(UP + 2 * g, 256, stride=16), :] = y[:, :128]
        gm_o[pl.ds(UP + 2 * g + 1, 256, stride=16), :] = y[:, 128:]
    vput("g2", col_sum(dq2 * n2))
    vput("h2", col_sum(dq2))
    vput("u_bo", c32[DVW + 256 : DVW + 257, :])
    vput("h4", sum(c32[G1 + 64 * b + 57 : G1 + 64 * b + 58, :] * a32[WT + b : WT + b + 1, :] for b in range(4)))
    vput("g4", sum(col_sum(c32[DGAIN + 8 * b : DGAIN + 8 * b + 8, :]) * a32[WT + b : WT + b + 1, :] for b in range(4)))
    pack256(gm_o, UO, mm3(expand(v2, m128), c32[DVW : DVW + 256, :], 0, 0))
    k2x = expand(k2, m128)
    gm_o[UQ : UQ + 256, :] = mm3(c32[DM2 : DM2 + 256, :], k2x) * scale1
    vput("u_bq", mm3(jnp.broadcast_to(c32[DC2 : DC2 + 1, :], (8, 256)), k2x)[0:1] * scale1)
    gm_o[UK : UK + 256, :] = outer(q3 + pe, dk2)
    gm_o[UV : UV + 256, :] = outer(q3, dv2)
    vput("u_bv", col_sum(dv2))
    vput("t_bo", col_sum(dx2))
    pack256(gm_o, TO, outer(mixed, dx2))
    vput("t_bv", col_sum(dmixed))
    gm_o[TV : TV + 256, :] = mm3(a32[U1 : U1 + 256, :], expand(dmixed, m128), 0, 0)
    dft = c32[DF1 : DF1 + 256, :]
    gm_o[TK : TK + 256, :] = mm3(dft, expand(b32[NAR : NAR + 32, :], m128)) * scale1
    dqt = collapse(mm_w(dft.T, slim[1]), m128) * scale1 * live_rows(INNER)
    vput("t_bq", col_sum(dqt))
    m, q0, q, k, v, o, n1, q1 = (tok32(a32, TOK, i) for i in range(8))
    gm_o[TQ : TQ + 256, :] = outer(q1 + pe, dqt)
    dq1 = dx2 + mm_w(dqt, slim[0], 1)
    vput("g1", col_sum(dq1 * n1))
    vput("h1", col_sum(dq1))
    dx1 = ln_back(dq1, n1, b32[RR : RR + 32, 0:1], vget(vec, "g1"))
    m256 = head_mask(D)
    scale = 1.0 / math.sqrt(D // HEADS)
    weights.wait()
    vput("s_bo", col_sum(dx1))
    pack256(gm_o, SO, outer(o, dx1))
    do = expand(mm_w(dx1, self_i[768:1024, :], 1), m256)
    p = b32[PS : PS + 256, 0:32]
    dv = mm3(p, do, 0, 0)
    dp = mm3(do, v, 1, 1)
    ds = p * (dp - jnp.sum(p * dp, axis=1, keepdims=True))
    dq = collapse(mm3(ds, k), m256) * scale
    dk = mm3(ds, expand(q, m256), 0, 0) * scale
    vput("s_bq", col_sum(dq))
    vput("s_bv", col_sum(dv))
    pack256(gm_o, SQ, outer(m, dq))
    pack256(gm_o, SK, outer(m, dk))
    pack256(gm_o, SV, outer(q0, dv))
    dq_o[...] = dx1 + mm_w(dq, self_i[0:256, :], 1) + mm_w(dk, self_i[256:512, :], 1) + mm_w(dv, self_i[512:768, :], 1)
    core = place[1]

    def hand(p, carry):
        for ref, c in ((mine_o, core), (other_o, 1 - core)):
            ref[p] = gm_o[pl.ds(chunk_row(p, c), CHUNK), :]
        return carry

    lax.fori_loop(0, PEERS, hand, 0, unroll=2)


def param_grads(*args):
    return pl.pallas_call(
        grads_kernel,
        in_specs=[pl.BlockSpec(memory_space=pltpu.SMEM)]
        + in_vmem(len(args) - 2)
        + [pl.BlockSpec(memory_space=pl.ANY)],
        out_specs=in_vmem(3),
        scratch_shapes=[
            pltpu.VMEM((PADDED, 128), F32),
            pltpu.VMEM((1024, 256), BF),
            pltpu.SemaphoreType.DMA,
        ],
        out_shape=specs([((PEERS, CHUNK, 128), F32), ((PEERS, CHUNK, 128), F32), ((32, 256), F32)]),
        compiler_params=pltpu.CompilerParams(vmem_limit_bytes=12 * MIB),
        cost_estimate=pl.CostEstimate(flops=2 * 10**10, bytes_accessed=10**4, transcendentals=0),
        name="param_grads",
    )(*args)


def merged(x):
    row = iota((CHUNK, 128), 0)
    q, k = fixed(x, 0)
    return jnp.where(row == CHUNK - 1, k.astype(jnp.int32), q).astype(jnp.int16)


def merge_kernel(a, b, out):
    def some(p, carry):
        out[p] = merged(a[p] + b[p])
        return carry

    lax.fori_loop(0, PEERS, some, 0, unroll=4)


def merge(a, b):
    return pl.pallas_call(
        merge_kernel,
        in_specs=in_vmem(2),
        out_specs=in_vmem(1)[0],
        out_shape=jax.ShapeDtypeStruct((PEERS, CHUNK, 128), jnp.int16),
        compiler_params=pltpu.CompilerParams(vmem_limit_bytes=4 * MIB),
        name="merge",
    )(a, b)


def settle_kernel(where, came, m, one, two, one_o, two_o, up_o, sq_o):
    def some(i, total):
        for p in range(4):
            x = came[4 * i + p].astype(F32)
            total = total + x * jnp.exp2(x[CHUNK - 1 :, :])
        return total

    g = lax.fori_loop(0, PEERS // 4, some, jnp.zeros((CHUNK, 128), F32))
    master = m[...]
    first = 0.5 * one[...] + 0.5 * g
    second = 0.5 * two[...] + 0.5 * g * g
    fix = 1.0 - 0.5**STEP
    update = first / fix / (jnp.sqrt(second / fix) + 1e-06) + 0.01 * master
    one_o[...] = first
    two_o[...] = second
    up_o[...] = update
    at = iota((CHUNK, 128), 0) * 128 + iota((CHUNK, 128), 1)
    start, cut, end, piece = (where[k] for k in range(4))
    lane = iota((1, 128), 1)
    line = jnp.zeros((1, 128), F32)
    for k, x in enumerate((master, update)):
        sq = x * x
        for lo, hi, slot in ((start, cut, piece), (cut, end, piece + 1)):
            part = jnp.where((at >= lo) & (at < hi), sq, 0.0)
            part = jnp.sum(col_sum(part), axis=1, keepdims=True)
            line = line + jnp.where(lane == slot + 64 * k, part, 0.0)
    sq_o[...] = jnp.broadcast_to(line[None], (2 * PEERS, 1, 128))


def settle(where, came, m, one, two):
    chunk = jax.ShapeDtypeStruct((CHUNK, 128), F32)
    return pl.pallas_call(
        settle_kernel,
        in_specs=[pl.BlockSpec(memory_space=pltpu.SMEM)] + in_vmem(4),
        out_specs=in_vmem(4),
        out_shape=[chunk, chunk, chunk, jax.ShapeDtypeStruct((2 * PEERS, 1, 128), F32)],
        compiler_params=pltpu.CompilerParams(vmem_limit_bytes=4 * MIB),
        name="settle",
    )(where, came, m, one, two)


def rates():
    order = jnp.arange(D // 2, dtype=F32)
    radius = 1.0 + jnp.mod(order, 4.0)
    turn = order * 2.39996
    return 2.0 * math.pi * radius * jnp.cos(turn), 2.0 * math.pi * radius * jnp.sin(turn)


def token_pe(coords):
    along, down = rates()
    points = (coords.astype(F32) + 0.5) / 1024.0 * 2.0 - 1.0
    points = points.reshape(4, 2, 2)
    phase = points[..., 0:1] * along + points[..., 1:2] * down
    corner = jnp.concatenate([jnp.sin(phase), jnp.cos(phase)], axis=-1)
    corner = jnp.swapaxes(corner, 0, 1).reshape(8, D)
    return jnp.concatenate([jnp.zeros((20, D), F32), corner, jnp.zeros((4, D), F32)], axis=0)


def by_token(x):
    y = jnp.swapaxes(x, 0, 1).reshape(4 * QT, x.shape[-1])
    return jnp.concatenate([y, jnp.zeros((4, x.shape[-1]), y.dtype)], axis=0)


def by_box(x):
    return jnp.swapaxes(x[: 4 * QT].reshape(QT, 4, x.shape[-1]), 0, 1)


def device_work(place, own, peer, queries, coords, cot_q, cot_k, mine, swap):
    along, down = rates()
    cells = jnp.arange(GRID, dtype=F32)
    across = 2.0 * (cells + 0.5) / GRID - 1.0
    line = jnp.mod(jnp.arange(GRID, dtype=jnp.int32) + place[0] * (GRID // 2), GRID).astype(F32)
    below = 2.0 * (line + 0.5) / GRID - 1.0
    pa = across[:, None] * along[None, :]
    pb = below[:, None] * down[None, :]
    tables = (jnp.sin(pa), jnp.cos(pa), jnp.sin(pb), jnp.cos(pb))
    ready = prep(peer, HALF, *tables, filled=prep(own, 0, *tables))
    pe = token_pe(coords)
    q0 = by_token(queries.astype(F32))
    cq = by_token(cot_q.astype(F32))
    place, ready, pe, q0, cq, mine = lax.optimization_barrier((place, ready, pe, q0, cq, mine))
    k0, lh, ll, lht, llt, k0t = ready
    s1, big, a32, b32, w16, slim = tokens(place, q0, pe, mine, swap(mine), lh, ll, k0t)
    keys, img, one, two, three, c32 = image_side(
        place, cot_k, k0, lh, ll, lht, llt, s1, big, cq, a32, b32, w16, slim
    )
    parts = one, two, three
    gmine, gother, dq = param_grads(place, pe, a32, b32, slim, c32, w16)
    queries_out = a32[TOK2 + 96 : TOK2 + 128]
    return by_box(queries_out).astype(BF), keys, by_box(dq), img, parts, gmine, gother


SWAP = [(0, 1), (1, 0)]
HALFWAY = ("cuts_0", "cuts_1", "cuts_2", "box")
RING_Y = ("cuts_1", "box")


def passed(x, axis, step):
    return lax.ppermute(x, axis, [(i, (i + step) % 4) for i in range(4)])


def ring_all(x, axis):
    return [x, passed(x, axis, 1), passed(x, axis, -1), passed(x, axis, 2)]


def swap(x):
    return lax.ppermute(x, "cuts_3", SWAP)


def local(
    queries_in, image, box_coords, box_mask, volume_ids, cot_queries, cot_keys, master, moment1, moment2,
):
    box = lax.axis_index("box")
    me = lax.axis_index(CUTS_BOX)
    own = image[0]
    shard = master.shape[0]
    first_row = ((771 * me) // 64) * 8
    shift = shard * me - 128 * first_row
    peer = lax.ppermute(own, "box", SWAP)
    room = 1024
    long = jnp.concatenate(
        [jnp.zeros((room,), BF), master.astype(BF), jnp.zeros((CHUNK * 128 - shard,), BF)]
    )
    chunk = lax.dynamic_slice(long, (room - shift,), (CHUNK * 128,)).reshape(CHUNK, 128)
    last = jnp.concatenate([box_mask[0].astype(BF), volume_ids.astype(BF), jnp.zeros((123,), BF)])
    chunk = jnp.where(jnp.arange(CHUNK, dtype=jnp.int32)[:, None] == CHUNK - 1, last[None], chunk)
    column = jnp.stack(ring_all(chunk, RING_Y))
    plane = lax.all_to_all(
        jnp.broadcast_to(column[None], (PEERS // 4, 4, CHUNK, 128)), ("cuts_0", "cuts_2"), 0, 0, tiled=True
    )
    mine = plane.reshape(PEERS, CHUNK, 128)
    place = jnp.concatenate(
        [
            jnp.stack([box, lax.axis_index("cuts_3"), 2 * lax.axis_index("cuts_1") + box, volume_ids[0]]),
            box_mask[0],
        ]
    ).astype(jnp.int32)

    queries_out, keys_out, queries_grad, img, parts, gmine, gother = device_work(
        place, own, peer, queries_in[0], box_coords[0], cot_queries[0], cot_keys[0], mine, swap
    )
    one, two, three = parts
    one = lax.ppermute(one, "box", SWAP)
    gother, one, two = lax.optimization_barrier((gother, one, two))
    two = lax.ppermute(two, "box", SWAP)

    start = shard * me
    edges = jnp.array([128 * r for r in ROW0[1:]], jnp.int32)
    piece = jnp.sum((edges <= start).astype(jnp.int32))
    edge = functools.reduce(
        lambda e, r: jnp.where((128 * r > start) & (e > 128 * r), 128 * r, e), ROW0[1:], start + shard
    )
    cut = jnp.minimum(edge, start + shard) - start

    def laid(x):
        return lax.dynamic_update_slice(jnp.zeros((CHUNK * 128,), F32), x, (shift,)).reshape(CHUNK, 128)

    def taken(x):
        return lax.dynamic_slice(x.reshape(CHUNK * 128), (shift,), (shard,))

    states = [laid(x) for x in (master, moment1, moment2)]
    sent = merge(gmine, swap(gother))
    sent, two, img = lax.optimization_barrier((sent, two, img))
    came = lax.all_to_all(sent, HALFWAY, 0, 0, tiled=True)
    img = land(land(img, one, PART0[0]), two, PART0[1])
    where = jnp.stack([shift, shift + cut, shift + shard, piece]).astype(jnp.int32)
    came, three, img, states, where = lax.optimization_barrier((came, three, img, states, where))
    three = lax.ppermute(three, "box", SWAP)
    new_first, new_second, update, squares = settle(where, came, *states)
    squares = lax.all_to_all(squares, CUTS_BOX, 0, 0, tiled=True)
    new_first, new_second, update = taken(new_first), taken(new_second), taken(update)
    image_grad = land(img, three, PART0[2])
    squares, image_grad = lax.optimization_barrier((squares, image_grad))
    squares = jnp.sum(squares, axis=(0, 1))
    weight_norm = jnp.sqrt(squares[:14])
    update_norm = jnp.sqrt(squares[64:78])
    ratio = jnp.concatenate([weight_norm / (update_norm + 1e-06), jnp.ones((2,), F32)])
    entry = jnp.where(jnp.arange(shard, dtype=jnp.int32) < cut, ratio[piece], ratio[piece + 1])
    new_master = master - 0.25 * entry * update
    return (
        queries_out[None],
        keys_out[None],
        queries_grad[None],
        image_grad[None],
        new_master,
        new_first,
        new_second,
        new_master.astype(BF),
        jnp.stack([weight_norm, update_norm]),
    )


def solution(mesh):
    torus = Mesh(
        mesh.devices.reshape(4, 2, 4, 2, mesh.shape["box"]),
        ("cuts_0", "cuts_1", "cuts_2", "cuts_3", "box"),
    )
    in_specs = (
        P(CUTS, "box", None, None),
        P(CUTS, "box", None),
        P(CUTS, "box", None),
        P(CUTS, "box"),
        P(CUTS),
        P(CUTS, "box", None, None),
        P(CUTS, "box", None, None),
        P(CUTS_BOX),
        P(CUTS_BOX),
        P(CUTS_BOX),
    )
    out_specs = (
        P(CUTS, "box", None, None),
        P(CUTS, "box", None, None),
        P(CUTS, "box", None, None),
        P(CUTS, "box", None),
        P(CUTS_BOX),
        P(CUTS_BOX),
        P(CUTS_BOX),
        P(CUTS_BOX),
        P(),
    )
    return jax.shard_map(local, mesh=torus, in_specs=in_specs, out_specs=out_specs, check_vma=False)
```

```python
import functools
import math

import jax
import jax.numpy as jnp
from jax import lax
from jax.experimental import pallas as pl
from jax.experimental.pallas import tpu as pltpu
from jax.sharding import Mesh
from jax.sharding import PartitionSpec as P

D = 256
INNER = 128
FF = 2048
HEADS = 8
GRID = 64
QT = 7
STEP = 5
CUTS = ("cuts_0", "cuts_1", "cuts_2", "cuts_3")
CUTS_BOX = ("cuts_0", "cuts_1", "cuts_2", "cuts_3", "box")
F32 = jnp.float32
BF = jnp.bfloat16
NEG = -1e30

MROWS = 12288
VLEN = 6144
VROWS = VLEN // 128
CHUNK = 112
PADDED = 12352
PEERS = 64
MATRIX_ROWS = (512, 512, 512, 512, 256, 256, 256, 256, 256, 256, 256, 256, 4096, 4096)
ROW0 = tuple(sum(MATRIX_ROWS[:i]) for i in range(15))
(SQ, SK, SV, SO, TQ, TK, TV, TO, UQ, UK, UV, UO, UP, DOWN) = ROW0[:14]
VECTORS = (
    ("s_bq", 256), ("s_bv", 256), ("s_bo", 256), ("t_bq", 128), ("t_bv", 128), ("t_bo", 256),
    ("u_bq", 128), ("u_bv", 128), ("u_bo", 256), ("bup", 2048), ("bdown", 256),
    ("g1", 256), ("g2", 256), ("g3", 256), ("g4", 256),
    ("h1", 256), ("h2", 256), ("h3", 256), ("h4", 256),
)
VOFF = {}
_at = 0
for _name, _len in VECTORS:
    VOFF[_name] = (_at, _len)
    _at += _len

TC = 512
IMG = GRID * GRID
STEPS = IMG // TC
HALF = STEPS // 2
TI = 1024
STEPS_I = IMG // TI
HALF_I = STEPS_I // 2
SENT = TC + 16 * (TC // 256)
RB = 64
SB = 64
PART0 = (0, 1, 2)
MIB = 1024 * 1024
MOST = 58 * MIB
IMAGE = 55 * MIB


def mm(a, b, ca=1, cb=0):
    return lax.dot_general(a, b, (((ca,), (cb,)), ((), ())), preferred_element_type=F32)


def split(x):
    hi = x.astype(BF)
    return hi, (x - hi.astype(F32)).astype(BF)


def mm_w(x, w, cb=0):
    hi, lo = split(x)
    rows = x.shape[0]
    y = mm(jnp.concatenate([hi, lo], axis=0), w, 1, cb)
    return y[:rows] + y[rows:]


def mm3(a, b, ca=1, cb=0):
    ah, al = split(a)
    bh, bl = split(b)
    return mm(ah, bh, ca, cb) + (mm(ah, bl, ca, cb) + mm(al, bh, ca, cb))


def mm3s(ah, al, bh, bl, ca=1, cb=0):
    return mm(ah, bh, ca, cb) + (mm(ah, bl, ca, cb) + mm(al, bh, ca, cb))


def cat3(a, dim):
    hi, lo = split(a)
    return jnp.concatenate([hi, hi, lo], axis=dim)


def cat3r(a, dim):
    hi, lo = split(a)
    return jnp.concatenate([hi, lo, hi], axis=dim)


def outer(a, b):
    ah, al = split(a)
    bh, bl = split(b)
    left = jnp.concatenate([ah, al, ah], axis=0)
    right = jnp.concatenate([bh, bh, bl], axis=0)
    return mm(left, right, 0, 0)


def iota(shape, dim):
    return lax.broadcasted_iota(jnp.int32, shape, dim)


def head_mask(width):
    c = iota((256, width), 0) % HEADS
    e = iota((256, width), 1) // (width // HEADS)
    return (c == e).astype(F32)


def expand(x, mask):
    n = x.shape[1]
    return jnp.broadcast_to(x[:, None, :], (32, HEADS, n)).reshape(256, n) * mask


def collapse(y, mask):
    n = y.shape[1]
    return jnp.sum((y * mask).reshape(32, HEADS, n), axis=1)


def live_rows(n):
    return (iota((32, n), 0) < 4 * QT).astype(F32)


def ln(x, gain, shift):
    centered = x - jnp.mean(x, axis=-1, keepdims=True)
    r = lax.rsqrt(jnp.mean(centered * centered, axis=-1, keepdims=True) + 1e-5)
    n = centered * r
    return n * gain + shift, n, r


def ln_back(dy, n, r, gain):
    h = dy * gain
    m1 = jnp.mean(h, axis=-1, keepdims=True)
    m2 = jnp.mean(h * n, axis=-1, keepdims=True)
    return r * (h - m1 - n * m2)


def col_sum(x):
    return jnp.sum(x, axis=0, keepdims=True)


def vget(ref, name):
    at, n = VOFF[name]
    row = at // 128
    return jnp.concatenate([ref[row + k : row + k + 1, :] for k in range(n // 128)], axis=1)


def wide(ref, row, n):
    left = ref[pl.ds(row, n, stride=2), :].astype(BF)
    right = ref[pl.ds(row + 1, n, stride=2), :].astype(BF)
    return jnp.concatenate([left, right], axis=1)


def pack256(ref, row, x):
    n = x.shape[0]
    ref[pl.ds(row, n, stride=2), :] = x[:, :128]
    ref[pl.ds(row + 1, n, stride=2), :] = x[:, 128:]


def chunk_row(p, core):
    device = (p // 2) * 4 + core * 2 + p % 2
    return pl.multiple_of(((771 * device) // 64) * 8, 8)


def fixed(x, dim=1):
    top = jnp.max(jnp.abs(x), axis=dim, keepdims=True)
    power = jnp.ceil(jnp.log2(jnp.maximum(top, 1e-30))) - 14.0
    return jnp.round(x * jnp.exp2(-power)).astype(jnp.int32), power


def on_lanes(column, rows):
    n = column.shape[0]
    return jnp.broadcast_to(column, (n, 128)).T[:rows]


def gelu_parts(x):
    cdf = 0.5 * (1.0 + lax.erf(x * math.sqrt(0.5)))
    return cdf


def in_vmem(n):
    return [pl.BlockSpec(memory_space=pltpu.VMEM)] * n


def specs(shapes):
    return [jax.ShapeDtypeStruct(shape, t) for shape, t, *_ in shapes]


def prep_kernel(half, sa, ca, sb, cb, *refs):
    k0_o, lh_o, ll_o, lht_o, llt_o, k0t_o = refs[-6:]
    k0 = half[...]
    rows = []
    for q in range(TC // GRID):
        s, c = sb[q : q + 1, :], cb[q : q + 1, :]
        rows.append(
            jnp.concatenate([sa[...] * c + ca[...] * s, ca[...] * c - sa[...] * s], axis=1)
        )
    loc = k0.astype(F32) + jnp.concatenate(rows, axis=0)
    hi, lo = split(loc)
    k0_o[...] = k0
    lh_o[...] = hi
    ll_o[...] = lo
    lht_o[...] = hi.T
    llt_o[...] = lo.T
    k0t_o[...] = k0.T


def prep(half, at, sa, ca, sb, cb, filled=()):
    col = pl.BlockSpec((D, TC), lambda j: (0, j + at))
    row = pl.BlockSpec((TC, D), lambda j: (j + at, 0))
    full = pl.BlockSpec((GRID, 128), lambda j: (0, 0))
    part = pl.BlockSpec((TC // GRID, 128), lambda j: (j + at, 0))
    rs = jax.ShapeDtypeStruct((IMG, D), BF)
    cs = jax.ShapeDtypeStruct((D, IMG), BF)
    return pl.pallas_call(
        prep_kernel,
        grid=(HALF,),
        in_specs=[pl.BlockSpec((TC, D), lambda j: (j, 0)), full, full, part, part]
        + [pl.BlockSpec(memory_space=pl.ANY)] * len(filled),
        out_specs=[row, row, row, col, col, col],
        out_shape=[rs, rs, rs, cs, cs, cs],
        input_output_aliases={5 + i: i for i in range(len(filled))},
        compiler_params=pltpu.CompilerParams(vmem_limit_bytes=MOST),
        cost_estimate=pl.CostEstimate(flops=10**9, bytes_accessed=8 * 10**6, transcendentals=0),
        name="prep",
    )(half, sa, ca, sb, cb, *filled)


HOPS = (0, -1, 1, 2)

STAT, SMALL, WT, TOK, TOK2, F1, U1, PRE, ROWS32 = 0, 16, 32, 64, 320, 448, 704, 960, 1216
NAR, NAR2, RR, VEC, PS, NARROW32 = 0, 32, 128, 224, 272, 528
SELF, TOW, UOW, UPB, DOWNB, ROWS16 = 0, 1024, 1152, 1280, 3328, 5376

DM2, DF1, DPRE, DVW, DTOK, DNAR, DC2, DOTS, DGAIN, DSHIFT, ROWSC = 0, 256, 512, 768, 1032, 1160, 1256, 1264, 1272, 1304, 1312


def tok32(ref, row, k):
    return ref[row + 32 * k : row + 32 * k + 32, :]


def up_blocks(w):
    return [w[UPB + 256 * k : UPB + 256 * k + 256, :] for k in range(8)]


def lay_weights(place, pieces, w_s, notes_s):
    core, y0 = place[1], place[2]
    w_s[...] = jnp.zeros((PADDED, 128), F32)
    keep = (iota((8, 128), 0) < 7).astype(F32)
    for at, n, copies, refs in pieces:
        for copy in copies:
            copy.wait()

        def lay(p, carry, refs=refs):
            k = p % 4
            y = (y0 + jnp.where(k == 1, 3, jnp.where(k == 2, 1, jnp.where(k == 3, 2, 0)))) % 4
            for ref, c, seen in zip(refs, (core, 1 - core), (0, PEERS)):
                device = (p // 16) * 32 + (y // 2) * 16 + ((p // 4) % 4) * 4 + c * 2 + y % 2
                row = ((771 * device) // 64) * 8
                block = ref[p].astype(F32)
                for lo, hi in ((0, 16), (16, 96), (96, CHUNK - 8), (CHUNK - 8, CHUNK)):
                    to = pl.ds(pl.multiple_of(row + lo, 8), hi - lo)
                    part = block[lo:hi]
                    if hi == CHUNK:
                        part = part * keep
                    w_s[to, :] = part if lo == 16 else w_s[to, :] + part
                notes_s[pl.ds(seen + p, 1), :] = block[CHUNK - 1 :, :]
            return carry

        lax.fori_loop(at, at + n, lay, 0, unroll=2)


def tokens_kernel(
    place, q0_i, pe_i, mine_h, other_h, lh_h, ll_h, k0t_h,
    s1_h, big_h, a32_h, b32_h, w16_h, slim_h, wself_h,
    s1_o, big, a32, b32, w16, slim,
    w_s, notes_s, ut, mine_i, other_i, lh_i, ll_i, k0t_i, sems, sems_out,
):
    vec = b32.at[VEC : VEC + VROWS]
    leaving = []

    def leave(k, src, dst):
        copy = pltpu.make_async_copy(src, dst, sems_out.at[k])
        copy.start()
        leaving.append(copy)

    quarter = PEERS // 4
    pieces = []
    for k in range(4):
        part = pl.ds(k * quarter, quarter)
        copies = [
            pltpu.make_async_copy(src.at[part], dst.at[part], sems.at[2 * k + n])
            for n, (src, dst) in enumerate(((mine_h, mine_i), (other_h, other_i)))
        ]
        for copy in copies:
            copy.start()
        pieces.append((k * quarter, quarter, copies, (mine_i, other_i)))
    later = [
        pltpu.make_async_copy(src, dst, sems.at[8 + n])
        for n, (src, dst) in enumerate(((lh_h, lh_i), (ll_h, ll_i), (k0t_h, k0t_i)))
    ]
    for copy in later:
        copy.start()
    lay_weights(place, pieces, w_s, notes_s)
    notes = notes_s[...]
    same = notes[:, 4:5] == place[3].astype(F32)
    lane128 = iota((128, 128), 1)
    count = jnp.sum(col_sum(jnp.where(same & (lane128 < 4), notes, 0.0)), axis=1, keepdims=True)
    weights = [place[4 + b].astype(F32) / count for b in range(4)]
    a32[0:TOK, :] = jnp.zeros((TOK, 256), F32)
    for b in range(4):
        a32[WT + b : WT + b + 1, :] = jnp.broadcast_to(weights[b], (1, 256))
    vec[...] = w_s[MROWS : MROWS + VROWS, :]
    for k, at in enumerate((TQ, TK, TV, UQ, UK, UV)):
        slim[k] = w_s[at : at + 256, :].astype(BF)
    leave(0, slim, slim_h)
    for k, at in enumerate((SQ, SK, SV, SO)):
        w16[SELF + 256 * k : SELF + 256 * k + 256, :] = wide(w_s, at, 256)
    w16[TOW : TOW + 128, :] = wide(w_s, TO, 128)
    w16[UOW : UOW + 128, :] = wide(w_s, UO, 128)
    for k in range(16):
        at = UPB + 256 * (k // 2)
        lanes = slice(128 * (k % 2), 128 * (k % 2) + 128)
        w16[at : at + 256, lanes] = w_s[pl.ds(UP + k, 256, stride=16), :].astype(BF)
    for k in range(8):
        w16[DOWNB + 256 * k : DOWNB + 256 * k + 256, :] = wide(w_s, DOWN + 512 * k, 256)
    leave(2, w16, w16_h)
    leave(8, w16.at[SELF : SELF + 1024], wself_h)

    def self_w(k):
        return w16[SELF + 256 * k : SELF + 256 * k + 256, :]

    q0 = q0_i[...]
    pe = pe_i[...]
    m = q0 + pe
    q = mm_w(m, self_w(0)) + vget(vec, "s_bq")
    k = mm_w(m, self_w(1))
    v = mm_w(q0, self_w(2)) + vget(vec, "s_bv")
    m256 = head_mask(D)
    m128 = head_mask(INNER)
    qe = expand(q * (1.0 / math.sqrt(D // HEADS)), m256)
    s = mm3(qe, k, 1, 1)
    c = iota((256, 32), 0)
    r = iota((256, 32), 1)
    valid = ((c // HEADS) % 4 == r % 4) & (r < 4 * QT)
    s = jnp.where(valid, s, NEG)
    e = jnp.exp(s - jnp.max(s, axis=1, keepdims=True))
    p = e / jnp.sum(e, axis=1, keepdims=True)
    o = collapse(mm3(p, v), m256)
    a = mm_w(o, self_w(3)) + vget(vec, "s_bo")
    q1, n1, r1 = ln(q0 + a, vget(vec, "g1"), vget(vec, "h1"))
    qt = mm_w(q1 + pe, slim[0]) + vget(vec, "t_bq")
    qx = expand(qt * (1.0 / math.sqrt(INNER // HEADS)), m128)
    f1 = mm_w(qx, slim[1], 1)
    for at, x in enumerate((m, q0, q, k, v, o, n1, q1)):
        a32[TOK + 32 * at : TOK + 32 * at + 32, :] = x
    b32[NAR : NAR + 32, :] = qt
    b32[RR : RR + 32, :] = jnp.broadcast_to(r1, (32, 128))
    b32[PS : PS + 256, :] = jnp.concatenate([p, jnp.zeros((256, 96), F32)], axis=1)
    a32[F1 : F1 + 256, :] = f1
    f1t = cat3r(f1.T, 0)
    for copy in later:
        copy.wait()
    top = jnp.full((1, 256), NEG, F32)
    for j in range(STEPS_I):
        at = slice(j * TI, j * TI + TI)
        lh = lh_i[at, :]
        s1 = mm(jnp.concatenate([lh, lh, ll_i[at, :]], axis=1), f1t)
        s1_o[at, :] = s1
        top = jnp.maximum(top, jnp.max(s1, axis=0, keepdims=True))
    leave(1, s1_o, s1_h)
    total = jnp.zeros((1, 256), F32)
    for j in range(STEPS_I):
        at = slice(j * TI, j * TI + TI)
        e = jnp.exp(s1_o[at, :] - top)
        total = total + col_sum(e)
        eh, el = split(e)
        k0t = k0t_i[:, at]
        part = mm(jnp.concatenate([k0t, k0t], axis=1), jnp.concatenate([eh, el], axis=0))
        ut[...] = part if j == 0 else ut[...] + part
    inverse = 1.0 / total
    a32[STAT : STAT + 1, :] = top
    a32[STAT + 1 : STAT + 2, :] = inverse
    u1 = (ut[...] * inverse).T
    a32[U1 : U1 + 256, :] = u1
    mixed = collapse(mm_w(u1, slim[2]), m128) + vget(vec, "t_bv")
    a = mm_w(mixed, w16[TOW : TOW + 128, :]) + vget(vec, "t_bo")
    q2, n2, r2 = ln(q1 + a, vget(vec, "g2"), vget(vec, "h2"))
    pre = jnp.concatenate([mm_w(q2, w) for w in up_blocks(w16)], axis=1) + vget(vec, "bup")
    for k in range(8):
        a32[PRE + 32 * k : PRE + 32 * k + 32, :] = pre[:, 256 * k : 256 * k + 256]
    hid = pre * gelu_parts(pre)
    y = mm_w(hid, w16[DOWNB : DOWNB + FF, :]) + vget(vec, "bdown")
    q3, n3, r3 = ln(q2 + y, vget(vec, "g3"), vget(vec, "h3"))
    live = live_rows(INNER)
    k2 = mm_w(q3 + pe, slim[4]) * live
    v2 = (mm_w(q3, slim[5]) + vget(vec, "u_bv")) * live
    for at, x in enumerate((n2, q2, n3, q3)):
        a32[TOK2 + 32 * at : TOK2 + 32 * at + 32, :] = x
    leave(6, a32.at[TOK:ROWS32], a32_h.at[TOK:ROWS32])
    for at, x in enumerate((mixed, k2, v2)):
        b32[NAR2 + 32 * at : NAR2 + 32 * at + 32, :] = x
    b32[RR + 32 : RR + 64, :] = jnp.broadcast_to(r2, (32, 128))
    b32[RR + 64 : RR + 96, :] = jnp.broadcast_to(r3, (32, 128))
    leave(3, b32, b32_h)
    kx = expand(k2 * (1.0 / math.sqrt(INNER // HEADS)), m128)
    m2 = mm_w(kx, slim[3], 1)
    c2 = mm3(jnp.broadcast_to(vget(vec, "u_bq"), (8, INNER)), kx, 1, 1)[0:1, :]
    lane = iota((1, 256), 1)
    a32[SMALL : SMALL + 8, :] = jnp.broadcast_to(jnp.where(lane >= 224, NEG, c2), (8, 256))
    rows = iota((256, 1), 0)
    spare = (rows >= 224) & (rows % 8 == 0)
    big[0:768, :] = cat3r(jnp.where(spare, -1.0, m2), 0)
    big[768:1536, :] = cat3r(m2.T, 0)
    leave(7, big.at[0:BIG_W], big_h.at[0:BIG_W])
    vw = mm_w(expand(v2, m128), w16[UOW : UOW + 128, :])
    wc = vw - jnp.mean(vw, axis=1, keepdims=True)
    bo = vget(vec, "u_bo")
    bo = bo - jnp.mean(bo, axis=1, keepdims=True)
    wfull = jnp.where(spare, bo, wc)
    wh = wfull.astype(BF).astype(F32)
    wl = wfull - wh
    rolled = jnp.concatenate([wh[248:], wh[:248]], axis=0)
    low = jnp.concatenate([wl[240:], wl[:240]], axis=0)
    cls = (rows // 8) % 4
    wt = wc.T
    lane_cls = (lane // 8) % 4
    wth = wt.astype(BF).astype(F32)
    wtl = pltpu.roll(wt - wth, 8, 1)
    gain = vget(vec, "g4")
    gain_col = jnp.broadcast_to(gain, (8, 256)).T[:, 0:1]
    row_o = a32.at[SMALL + 8 : SMALL + 16]
    for b in range(4):
        ws = jnp.where(
            cls == b, wh, jnp.where(cls == (b + 1) % 4, rolled, jnp.where(cls == (b + 2) % 4, low, 0.0))
        )
        big[BIG_W + 256 * b : BIG_W + 256 * b + 256, :] = ws.astype(BF)
        scaled = gain_col * weights[b]
        a = jnp.where(lane == 224 + 8 * b, scaled * (1.0 / D), wt * scaled)
        ah = a.astype(BF).astype(F32)
        al = pltpu.roll(a - ah, 8, 1)
        at = BIG_A + 1024 * (b % 2) + 512 * (b // 2)
        big[at : at + 256, :] = jnp.where(
            lane_cls == b, ah, jnp.where(lane_cls == (b + 1) % 4, al, 0.0)
        ).astype(BF)
        big[at + 256 : at + 512, :] = jnp.where(
            lane_cls == b, -wth, jnp.where(lane_cls == (b + 1) % 4, -wtl, 0.0)
        ).astype(BF)
        row_o[b : b + 1, :] = gain * weights[b]
    row_o[4:5, :] = gain
    row_o[5:6, :] = vget(vec, "h4")
    leave(4, big.at[BIG_W:BIG], big_h.at[BIG_W:BIG])
    leave(5, a32.at[0:TOK], a32_h.at[0:TOK])
    for copy in leaving:
        copy.wait()


BIG_W = 1536
BIG_A = BIG_W + 1024
BIG = BIG_A + 2048


def tokens(place, q0, pe, mine, other, lh, ll, k0t):
    out = [
        ((IMG, 256), F32),
        ((BIG, 256), BF),
        ((ROWS32, 256), F32),
        ((NARROW32, 128), F32),
        ((ROWS16, 256), BF),
        ((6, 256, 128), BF),
    ]
    return pl.pallas_call(
        tokens_kernel,
        in_specs=[pl.BlockSpec(memory_space=pltpu.SMEM)]
        + in_vmem(2)
        + [pl.BlockSpec(memory_space=pl.ANY)] * 5,
        out_specs=[pl.BlockSpec(memory_space=pl.ANY)] * (len(out) + 1),
        out_shape=specs(out + [((1024, 256), BF)]),
        scratch_shapes=[pltpu.VMEM(shape, t) for shape, t in out]
        + [
            pltpu.VMEM((PADDED, 128), F32),
            pltpu.VMEM((2 * PEERS, 128), F32),
            pltpu.VMEM((256, 256), F32),
            pltpu.VMEM((PEERS, CHUNK, 128), BF),
            pltpu.VMEM((PEERS, CHUNK, 128), BF),
            pltpu.VMEM((IMG, D), BF),
            pltpu.VMEM((IMG, D), BF),
            pltpu.VMEM((D, IMG), BF),
            pltpu.SemaphoreType.DMA((11,)),
            pltpu.SemaphoreType.DMA((len(out) + 3,)),
        ],
        compiler_params=pltpu.CompilerParams(vmem_limit_bytes=MOST),
        cost_estimate=pl.CostEstimate(flops=2 * 10**10, bytes_accessed=3 * 10**7, transcendentals=0),
        name="tokens",
    )(place, q0, pe, mine, other, lh, ll, k0t)


def group_max(x):
    m = jnp.maximum(x[:, :128], x[:, 128:])
    m = jnp.maximum(m, pltpu.roll(m, 64, 1))
    return jnp.maximum(m, pltpu.roll(m, 32, 1))


def group_sum(x):
    m = x[:, :128] + x[:, 128:]
    m = m + pltpu.roll(m, 64, 1)
    return m + pltpu.roll(m, 32, 1)


def twice(m):
    return jnp.concatenate([m, m], axis=1)


def image_kernel(
    place, cot_i, k0_i, lh_i, ll_i, lht_i, llt_i, s1_i, big_i, small_i, cq_i, *refs,
):
    late_refs, held, sems = refs[:4], refs[-5:-1], refs[-1]
    a32, b32, w16, slim = held
    later = [pltpu.make_async_copy(src, dst, sems.at[k]) for k, (src, dst) in enumerate(zip(late_refs, held))]
    image_steps(
        place, cot_i, k0_i, lh_i, ll_i, lht_i, llt_i, s1_i, big_i, small_i, cq_i, a32, b32, w16, slim, later, *refs[4:-5]
    )


def image_steps(
    place, cot_i, k0_i, lh_i, ll_i, lht_i, llt_i, s1_i, big_i, small_i, cq_i, a32, b32, w16, slim, later,
    keys_o, img_o, part0_o, part1_o, part2_o, c32,
    s_s, p_s, left_s, b_s, n_s, r_s, x_s, kc_s, acc, g1_o, g2_o, dut, both,
):
    j = pl.program_id(0)

    @pl.when(j == 0)
    def _():
        for copy in later:
            copy.start()
        c32[...] = jnp.zeros((ROWSC, 256), F32)
        g1_o[...] = jnp.zeros(g1_o.shape, F32)
        g2_o[...] = jnp.zeros(g2_o.shape, F32)

    @pl.when(j < STEPS_I)
    def _():
        image_part(
            cot_i, k0_i, lh_i, ll_i, lht_i, llt_i, big_i, small_i, keys_o,
            acc.at[pl.ds(pl.multiple_of(j * TI, TI), TI)], c32, g1_o, g2_o,
            s_s, p_s, left_s, b_s, n_s, r_s, x_s, kc_s,
        )

    @pl.when(j == STEPS_I)
    def _():
        for copy in later:
            copy.wait()
        chain_part(cq_i, a32, b32, w16, slim, c32, g1_o, g2_o, dut, both)

    def step(at, keep):
        image_step(
            s1_i, k0_i, lht_i, llt_i, acc.at[at * TI : at * TI + TI], a32, dut, both,
            c32.at[DOTS : DOTS + 8], c32.at[DF1 : DF1 + 256], keep,
        )

    def keep_send(refs, n, img):
        send(refs[n], img)

    def keep_own(n, img):
        img_o[n * TC : n * TC + TC, :] = img

    for n, refs in enumerate(((part0_o, part1_o), (part2_o.at[0:SENT], part2_o.at[SENT:]))):
        pl.when(j == STEPS_I + n)(functools.partial(step, HALF_I + n, functools.partial(keep_send, refs)))
    for n in range(HALF_I):
        pl.when(j == STEPS_I + HALF_I + n)(functools.partial(step, n, keep_own))


def image_part(
    cot_i, k0_i, lh_i, ll_i, lht_i, llt_i, big_i, small_i, keys_o, acc_o, c32, g1_o, g2_o,
    s_s, p_s, left_s, b_s, n_s, r_s, x_s, kc_s,
):
    lh = lh_i[...]
    s_s[...] = mm(jnp.concatenate([lh, lh, ll_i[...]], axis=1), big_i[768:1536, :])
    lane = iota((SB, 256), 1)
    cls = (lane // 8) % 4
    for i in range(TI // SB):
        at = slice(i * SB, i * SB + SB)
        kf = k0_i[at, :].astype(F32)
        kc_s[at, :] = kf - jnp.mean(kf, axis=1, keepdims=True)
        s = s_s[at, :] + small_i[0:1, :]
        e = jnp.exp(s - twice(group_max(s)))
        p = e * twice(1.0 / group_sum(e))
        p = jnp.where((lane >= 224) & (lane % 8 == 0), 1.0, p)
        p_s[at, :] = p
        ph = p.astype(BF).astype(F32)
        plow = pltpu.roll(p - ph, 8, 1)
        pr = pltpu.roll(ph, 16, 1)
        for b in range(4):
            x = jnp.where(cls == b, ph, jnp.where(cls == (b + 1) % 4, plow, pr))
            left_s[b, at, :] = x.astype(BF)

    def product(b):
        b_s[b] = mm(left_s[b], big_i[BIG_W + 256 * b : BIG_W + 256 * b + 256, :])

    def box(b):
        for i in range(TI // RB):
            at = slice(i * RB, i * RB + RB)
            z = kc_s[at, :] + b_s[b, at, :]
            r = lax.rsqrt(jnp.mean(z * z, axis=1, keepdims=True) + 1e-5)
            n = z * r
            keys_o[b, at, :] = (n * small_i[12:13, :] + small_i[13:14, :]).astype(BF)
            g = cot_i[b, at, :].astype(F32)
            gn = g * n
            c32[DGAIN + 8 * b : DGAIN + 8 * b + 8, :] += jnp.sum(gn.reshape(RB // 8, 8, 256), axis=0)
            gain = small_i[8 + b : 9 + b, :]
            m2 = jnp.mean(gn * gain, axis=1, keepdims=True)
            nm = n * m2
            n_s[b, at, :] = nm.astype(BF)
            dz = r * (g * gain - nm)
            if b == 0:
                acc_o[at, :] = dz
            else:
                acc_o[at, :] += dz
            r_s[b, at, :] = jnp.broadcast_to(r, (RB, 128))

    def back_product(b):
        x_s[b] = mm(
            jnp.concatenate([cot_i[b], n_s[b], cot_i[b + 2], n_s[b + 2]], axis=1),
            big_i[BIG_A + 1024 * b : BIG_A + 1024 * b + 1024, :],
        )

    product(0)
    product(2)
    box(0)
    product(1)
    box(2)
    product(3)
    back_product(0)
    box(1)
    box(3)
    back_product(1)

    half = iota((SB, 128), 1)
    kind = (half // 8) % 4
    even = (lane // 8) % 2 == 0
    for i in range(TI // SB):
        at = slice(i * SB, i * SB + SB)
        rr = jnp.where(
            kind == 0,
            r_s[0, at, :],
            jnp.where(kind == 1, r_s[1, at, :], jnp.where(kind == 2, r_s[2, at, :], r_s[3, at, :])),
        )
        rr = twice(rr)
        xe = x_s[0, at, :]
        xo = x_s[1, at, :]
        x = jnp.where(even, xe, xo) + pltpu.roll(jnp.where(even, xo, xe), 248, 1)
        p = p_s[at, :]
        t = jnp.where(lane < 224, p, 0.0)
        dp = rr * x
        tdp = t * dp
        ds = tdp - t * twice(group_sum(tdp))
        s_s[at, :] = jnp.where((lane >= 224) & (lane % 8 == 0), dp, ds)
        p_s[at, :] = jnp.where((lane >= 224) & (lane % 8 == 1), 1.0, p * rr)

    ds = s_s[...]
    dh, dl = split(ds)
    acc_o[...] += mm(jnp.concatenate([dh, dh, dl], axis=1), big_i[0:768, :])
    lht = lht_i[...]
    c32[DM2 : DM2 + 256, :] += mm(
        jnp.concatenate([lht, llt_i[...], lht], axis=1), jnp.concatenate([dh, dh, dl], axis=0)
    )
    c32[DC2 : DC2 + 1, :] += col_sum(ds)
    l1 = p_s[...].T
    for b in range(4):
        pick = [l1[32 * i + 8 * b : 32 * i + 8 * b + 8] for i in range(8)]
        hi, lo = split(jnp.concatenate(pick, axis=0))
        y = mm(jnp.concatenate([hi, lo], axis=0), cot_i[b])
        g1_o[b] += y[:64] + y[64:]
        g2_o[b] += mm(hi, n_s[b])


def image_side(place, cot, k0, lh, ll, lht, llt, s1, big, cq, a32, b32, w16, slim):
    def const(*shape):
        return pl.BlockSpec(shape, lambda j, place: (0,) * len(shape))

    def once(*shape):
        return pl.BlockSpec(shape, lambda j, place: (0,) * len(shape), pipeline_mode=pl.Buffered(1))

    def now(j):
        return jnp.minimum(j, STEPS_I - 1)

    def again(j):
        return jnp.where(j < STEPS_I, j, lax.rem(j + HALF_I, STEPS_I))

    row = pl.BlockSpec((TI, D), lambda j, place: (now(j), 0))
    row2 = pl.BlockSpec((TI, D), lambda j, place: (again(j), 0))
    col2 = pl.BlockSpec((D, TI), lambda j, place: (0, again(j)))
    late = pl.BlockSpec((TI, D), lambda j, place: (jnp.where(j < STEPS_I, HALF_I, again(j)), 0))
    boxes = pl.BlockSpec((4, TI, D), lambda j, place: (0, lax.rem(now(j) + place[0] * HALF_I, STEPS_I), 0))
    own = pl.BlockSpec((TI, D), lambda j, place: (jnp.maximum(j - STEPS_I - HALF_I, 0), 0))
    out = [
        ((4, IMG, D), BF, boxes),
        ((IMG // 2, D), F32, own),
        ((SENT, D), jnp.int16, None),
        ((SENT, D), jnp.int16, None),
        ((2 * SENT, D), jnp.int16, None),
        ((ROWSC, 256), F32, None),
    ]
    whole = [a32, b32, w16, slim]
    return pl.pallas_call(
        image_kernel,
        grid_spec=pltpu.PrefetchScalarGridSpec(
            num_scalar_prefetch=1,
            grid=(2 * STEPS_I,),
            in_specs=[boxes, row2, row, row, col2, col2, late, once(*big.shape)]
            + [pl.BlockSpec((16, 256), lambda j, place: (SMALL // 16, 0)), once(*cq.shape)]
            + [pl.BlockSpec(memory_space=pl.ANY)] * len(whole),
            out_specs=[s if s is not None else const(*shape) for shape, _, s in out],
            scratch_shapes=[
                pltpu.VMEM((TI, 256), F32),
                pltpu.VMEM((TI, 256), F32),
                pltpu.VMEM((4, TI, 256), BF),
                pltpu.VMEM((4, TI, 256), F32),
                pltpu.VMEM((4, TI, 256), BF),
                pltpu.VMEM((4, TI, 128), F32),
                pltpu.VMEM((2, TI, 256), F32),
                pltpu.VMEM((TI, 256), F32),
                pltpu.VMEM((IMG, 256), F32),
                pltpu.VMEM((4, 64, 256), F32),
                pltpu.VMEM((4, 64, 256), F32),
                pltpu.VMEM((512, 256), BF),
                pltpu.VMEM((1536, 256), BF),
            ]
            + [pltpu.VMEM(x.shape, x.dtype) for x in whole]
            + [pltpu.SemaphoreType.DMA((len(whole),))],
        ),
        out_shape=specs(out),
        compiler_params=pltpu.CompilerParams(vmem_limit_bytes=IMAGE),
        cost_estimate=pl.CostEstimate(flops=5 * 10**10, bytes_accessed=4 * 10**7, transcendentals=0),
        name="image_side",
    )(place, cot, k0, lh, ll, lht, llt, s1, big, a32, cq, *whole)


def image_step(s1_i, k0_i, lht_i, llt_i, acc_i, stat_i, dut, both, dots, df1, keep):
    for n in range(TI // TC):
        at = slice(n * TC, n * TC + TC)
        k0 = k0_i[at, :]
        p = jnp.exp(s1_i[at, :] - stat_i[0:1, :]) * stat_i[1:2, :]
        dp = mm(jnp.concatenate([k0, k0], axis=1), dut[...])
        ds = p * (dp - dots[0:1, :])
        ph, plow = split(p)
        dh, dl = split(ds)
        img = acc_i[at, :] + mm(jnp.concatenate([ph, ph, plow, dh, dh, dl], axis=1), both[...])
        lht = lht_i[:, at]
        df1[...] += mm(
            jnp.concatenate([lht, llt_i[:, at], lht], axis=1), jnp.concatenate([dh, dh, dl], axis=0)
        )
        keep(n, img)


def send(ref, img):
    q, k = fixed(img)
    ref[0:TC, :] = q.astype(jnp.int16)
    k = on_lanes(k, 16).astype(jnp.int32).astype(jnp.int16)
    for part in range(TC // D):
        ref[TC + 16 * part : TC + 16 * part + 16, :] = k[:, D * part : D * part + D]


def chain_part(cq_i, a32, b32, w16, slim, c32, g1_i, g2_i, dut, both):
    m128 = head_mask(INNER)
    scale1 = 1.0 / math.sqrt(INNER // HEADS)
    vec = b32.at[VEC : VEC + VROWS]
    per_box = []
    for b in range(4):
        gain = a32[SMALL + 8 + b : SMALL + 9 + b, :]
        raw = g1_i[b]
        c32[DSHIFT + b : DSHIFT + b + 1, :] = raw[57:58]
        x = raw * gain - g2_i[b]
        per_box.append(x - jnp.mean(x, axis=1, keepdims=True))
    bo_sum = sum(x[56:57] for x in per_box)
    zero = jnp.zeros((8, 256), F32)
    dvw = jnp.concatenate(
        [per_box[b][8 * i : 8 * i + 8] if i < QT else zero for i in range(8) for b in range(4)],
        axis=0,
    )
    c32[DVW : DVW + 256, :] = dvw
    c32[DVW + 256 : DVW + 264, :] = jnp.broadcast_to(bo_sum, (8, 256))
    dv2 = collapse(mm_w(dvw, w16[UOW : UOW + 128, :], 1), m128)
    dc2_8 = jnp.broadcast_to(c32[DC2 : DC2 + 1, :], (8, 256))
    dk2x = mm_w(c32[DM2 : DM2 + 256, :].T, slim[3]) + dc2_8.T[:, 0:1] * vget(vec, "u_bq")
    dk2 = collapse(dk2x, m128) * scale1 * live_rows(INNER)
    box = iota((32, 1), 0) % 4
    weight = sum(jnp.where(box == b, a32[WT + b : WT + b + 1, 0:1], 0.0) for b in range(4))
    dq3 = cq_i[...] * weight + mm_w(dv2, slim[5], 1) + mm_w(dk2, slim[4], 1)
    dx3 = ln_back(dq3, tok32(a32, TOK2, 2), b32[RR + 64 : RR + 96, 0:1], vget(vec, "g3"))
    pre = jnp.concatenate([tok32(a32, PRE, k) for k in range(8)], axis=1)
    slope = gelu_parts(pre) + pre * (jnp.exp(-0.5 * pre * pre) * (1.0 / math.sqrt(2.0 * math.pi)))
    dpre = mm_w(dx3, w16[DOWNB : DOWNB + FF, :], 1) * slope
    dq2 = dx3 + sum(
        mm_w(dpre[:, 256 * k : 256 * k + 256], w, 1) for k, w in enumerate(up_blocks(w16))
    )
    dx2 = ln_back(dq2, tok32(a32, TOK2, 0), b32[RR + 32 : RR + 64, 0:1], vget(vec, "g2"))
    dmixed = mm_w(dx2, w16[TOW : TOW + 128, :], 1)
    du = mm_w(expand(dmixed, m128), slim[2], 1)
    dots = jnp.sum(du * a32[U1 : U1 + 256, :], axis=1, keepdims=True)
    c32[DOTS : DOTS + 8, :] = jnp.broadcast_to(dots, (256, 128)).T[0:8, :]
    duh, dul = split(du.T)
    dut[...] = jnp.concatenate([duh, dul], axis=0)
    both[...] = jnp.concatenate([cat3r(du, 0), cat3r(a32[F1 : F1 + 256, :], 0)], axis=0)
    for at, x in enumerate((dv2, dk2, dmixed)):
        c32[DNAR + 32 * at : DNAR + 32 * at + 32, 0:128] = x
    for at, x in enumerate((dq3, dx3, dq2, dx2)):
        c32[DTOK + 32 * at : DTOK + 32 * at + 32, :] = x
    for k in range(8):
        c32[DPRE + 32 * k : DPRE + 32 * k + 32, :] = dpre[:, 256 * k : 256 * k + 256]


def land_kernel(img, part, out):
    k = jnp.concatenate([part[TC + 16 * i : TC + 16 * i + 1, :] for i in range(TC // D)], axis=1)
    scale = jnp.exp2(jnp.broadcast_to(k.astype(F32), (8, TC)).T[:, 0:1])
    out[...] = img[...] + part[0:TC, :].astype(F32) * scale


def land(img, part, at):
    row = pl.BlockSpec((TC, D), lambda j: (j + at, 0))
    return pl.pallas_call(
        land_kernel,
        grid=(part.shape[0] // SENT,),
        in_specs=[row, pl.BlockSpec((SENT, D), lambda j: (j, 0))],
        out_specs=row,
        out_shape=jax.ShapeDtypeStruct(img.shape, F32),
        input_output_aliases={0: 0},
        compiler_params=pltpu.CompilerParams(vmem_limit_bytes=6 * MIB),
        name="land",
    )(img, part)


def vputter(ref, row0):
    def vput(name, x):
        at, n = VOFF[name]
        for k in range(n // 128):
            row = MROWS - row0 + at // 128 + k
            ref[row : row + 1, :] = x[:, 128 * k : 128 * k + 128]

    return vput


def grads_kernel(
    place, pe_i, a32, b32, slim, c32, self_i,
    mine_o, other_o, dq_o,
    gm_o,
):
    vec = b32.at[VEC : VEC + VROWS]
    m128 = head_mask(INNER)
    scale1 = 1.0 / math.sqrt(INNER // HEADS)
    vput = vputter(gm_o, 0)
    gm_o[MROWS:, :] = jnp.zeros((PADDED - MROWS, 128), F32)
    pe = pe_i[...]
    dv2, dk2, dmixed = (tok32(c32, DNAR, k)[:, 0:128] for k in range(3))
    dq3, dx3, dq2, dx2 = (tok32(c32, DTOK, k) for k in range(4))
    n2, q2, n3, q3 = (tok32(a32, TOK2, k) for k in range(4))
    mixed, k2, v2 = (tok32(b32, NAR2, k) for k in range(3))
    vput("g3", col_sum(dq3 * n3))
    vput("h3", col_sum(dq3))
    vput("bdown", col_sum(dx3))
    for g in range(8):
        pre = tok32(a32, PRE, g)
        pack256(gm_o, DOWN + 512 * g, outer(pre * gelu_parts(pre), dx3))
    dpre = [tok32(c32, DPRE, g) for g in range(8)]
    vput("bup", col_sum(jnp.concatenate(dpre, axis=1)))
    for g in range(8):
        y = outer(q2, dpre[g])
        gm_o[pl.ds(UP + 2 * g, 256, stride=16), :] = y[:, :128]
        gm_o[pl.ds(UP + 2 * g + 1, 256, stride=16), :] = y[:, 128:]
    vput("g2", col_sum(dq2 * n2))
    vput("h2", col_sum(dq2))
    vput("u_bo", c32[DVW + 256 : DVW + 257, :])
    vput("h4", sum(c32[DSHIFT + b : DSHIFT + b + 1, :] * a32[WT + b : WT + b + 1, :] for b in range(4)))
    vput("g4", sum(col_sum(c32[DGAIN + 8 * b : DGAIN + 8 * b + 8, :]) * a32[WT + b : WT + b + 1, :] for b in range(4)))
    pack256(gm_o, UO, mm3(expand(v2, m128), c32[DVW : DVW + 256, :], 0, 0))
    k2x = expand(k2, m128)
    gm_o[UQ : UQ + 256, :] = mm3(c32[DM2 : DM2 + 256, :], k2x) * scale1
    vput("u_bq", mm3(jnp.broadcast_to(c32[DC2 : DC2 + 1, :], (8, 256)), k2x)[0:1] * scale1)
    gm_o[UK : UK + 256, :] = outer(q3 + pe, dk2)
    gm_o[UV : UV + 256, :] = outer(q3, dv2)
    vput("u_bv", col_sum(dv2))
    vput("t_bo", col_sum(dx2))
    pack256(gm_o, TO, outer(mixed, dx2))
    vput("t_bv", col_sum(dmixed))
    gm_o[TV : TV + 256, :] = mm3(a32[U1 : U1 + 256, :], expand(dmixed, m128), 0, 0)
    dft = c32[DF1 : DF1 + 256, :]
    gm_o[TK : TK + 256, :] = mm3(dft, expand(b32[NAR : NAR + 32, :], m128)) * scale1
    dqt = collapse(mm_w(dft.T, slim[1]), m128) * scale1 * live_rows(INNER)
    vput("t_bq", col_sum(dqt))
    m, q0, q, k, v, o, n1, q1 = (tok32(a32, TOK, i) for i in range(8))
    gm_o[TQ : TQ + 256, :] = outer(q1 + pe, dqt)
    dq1 = dx2 + mm_w(dqt, slim[0], 1)
    vput("g1", col_sum(dq1 * n1))
    vput("h1", col_sum(dq1))
    dx1 = ln_back(dq1, n1, b32[RR : RR + 32, 0:1], vget(vec, "g1"))
    m256 = head_mask(D)
    scale = 1.0 / math.sqrt(D // HEADS)
    vput("s_bo", col_sum(dx1))
    pack256(gm_o, SO, outer(o, dx1))
    do = expand(mm_w(dx1, self_i[768:1024, :], 1), m256)
    p = b32[PS : PS + 256, 0:32]
    dv = mm3(p, do, 0, 0)
    dp = mm3(do, v, 1, 1)
    ds = p * (dp - jnp.sum(p * dp, axis=1, keepdims=True))
    dq = collapse(mm3(ds, k), m256) * scale
    dk = mm3(ds, expand(q, m256), 0, 0) * scale
    vput("s_bq", col_sum(dq))
    vput("s_bv", col_sum(dv))
    pack256(gm_o, SQ, outer(m, dq))
    pack256(gm_o, SK, outer(m, dk))
    pack256(gm_o, SV, outer(q0, dv))
    dq_o[...] = dx1 + mm_w(dq, self_i[0:256, :], 1) + mm_w(dk, self_i[256:512, :], 1) + mm_w(dv, self_i[512:768, :], 1)
    core = place[1]

    def hand(p, carry):
        for ref, c in ((mine_o, core), (other_o, 1 - core)):
            ref[p] = gm_o[pl.ds(chunk_row(p, c), CHUNK), :]
        return carry

    lax.fori_loop(0, PEERS, hand, 0, unroll=2)


def param_grads(*args):
    return pl.pallas_call(
        grads_kernel,
        in_specs=[pl.BlockSpec(memory_space=pltpu.SMEM)]
        + in_vmem(len(args) - 1),
        out_specs=in_vmem(3),
        scratch_shapes=[pltpu.VMEM((PADDED, 128), F32)],
        out_shape=specs([((PEERS, CHUNK, 128), F32), ((PEERS, CHUNK, 128), F32), ((32, 256), F32)]),
        compiler_params=pltpu.CompilerParams(vmem_limit_bytes=12 * MIB),
        cost_estimate=pl.CostEstimate(flops=2 * 10**10, bytes_accessed=10**4, transcendentals=0),
        name="param_grads",
    )(*args)


def merged(x):
    row = iota((CHUNK, 128), 0)
    q, k = fixed(x, 0)
    return jnp.where(row == CHUNK - 1, k.astype(jnp.int32), q).astype(jnp.int16)


def merge_kernel(a, b, out):
    def some(p, carry):
        out[p] = merged(a[p] + b[p])
        return carry

    lax.fori_loop(0, PEERS, some, 0, unroll=4)


def merge(a, b):
    return pl.pallas_call(
        merge_kernel,
        in_specs=in_vmem(2),
        out_specs=in_vmem(1)[0],
        out_shape=jax.ShapeDtypeStruct((PEERS, CHUNK, 128), jnp.int16),
        compiler_params=pltpu.CompilerParams(vmem_limit_bytes=4 * MIB),
        name="merge",
    )(a, b)


def settle_kernel(where, came, m, one, two, one_o, two_o, up_o, sq_o):
    def some(i, total):
        for p in range(4):
            x = came[4 * i + p].astype(F32)
            total = total + x * jnp.exp2(x[CHUNK - 1 :, :])
        return total

    g = lax.fori_loop(0, PEERS // 4, some, jnp.zeros((CHUNK, 128), F32))
    master = m[...]
    first = 0.5 * one[...] + 0.5 * g
    second = 0.5 * two[...] + 0.5 * g * g
    fix = 1.0 - 0.5**STEP
    update = first / fix / (jnp.sqrt(second / fix) + 1e-06) + 0.01 * master
    one_o[...] = first
    two_o[...] = second
    up_o[...] = update
    at = iota((CHUNK, 128), 0) * 128 + iota((CHUNK, 128), 1)
    start, cut, end, piece = (where[k] for k in range(4))
    lane = iota((1, 128), 1)
    line = jnp.zeros((1, 128), F32)
    for k, x in enumerate((master, update)):
        sq = x * x
        for lo, hi, slot in ((start, cut, piece), (cut, end, piece + 1)):
            part = jnp.where((at >= lo) & (at < hi), sq, 0.0)
            part = jnp.sum(col_sum(part), axis=1, keepdims=True)
            line = line + jnp.where(lane == slot + 64 * k, part, 0.0)
    sq_o[...] = jnp.broadcast_to(line[None], (2 * PEERS, 1, 128))


def settle(where, came, m, one, two):
    chunk = jax.ShapeDtypeStruct((CHUNK, 128), F32)
    return pl.pallas_call(
        settle_kernel,
        in_specs=[pl.BlockSpec(memory_space=pltpu.SMEM)] + in_vmem(4),
        out_specs=in_vmem(4),
        out_shape=[chunk, chunk, chunk, jax.ShapeDtypeStruct((2 * PEERS, 1, 128), F32)],
        compiler_params=pltpu.CompilerParams(vmem_limit_bytes=4 * MIB),
        name="settle",
    )(where, came, m, one, two)


def rates():
    order = jnp.arange(D // 2, dtype=F32)
    radius = 1.0 + jnp.mod(order, 4.0)
    turn = order * 2.39996
    return 2.0 * math.pi * radius * jnp.cos(turn), 2.0 * math.pi * radius * jnp.sin(turn)


def token_pe(coords):
    along, down = rates()
    points = (coords.astype(F32) + 0.5) / 1024.0 * 2.0 - 1.0
    points = points.reshape(4, 2, 2)
    phase = points[..., 0:1] * along + points[..., 1:2] * down
    corner = jnp.concatenate([jnp.sin(phase), jnp.cos(phase)], axis=-1)
    corner = jnp.swapaxes(corner, 0, 1).reshape(8, D)
    return jnp.concatenate([jnp.zeros((20, D), F32), corner, jnp.zeros((4, D), F32)], axis=0)


def by_token(x):
    y = jnp.swapaxes(x, 0, 1).reshape(4 * QT, x.shape[-1])
    return jnp.concatenate([y, jnp.zeros((4, x.shape[-1]), y.dtype)], axis=0)


def by_box(x):
    return jnp.swapaxes(x[: 4 * QT].reshape(QT, 4, x.shape[-1]), 0, 1)


def device_work(place, own, peer, queries, coords, cot_q, cot_k, mine, swap):
    along, down = rates()
    cells = jnp.arange(GRID, dtype=F32)
    across = 2.0 * (cells + 0.5) / GRID - 1.0
    line = jnp.mod(jnp.arange(GRID, dtype=jnp.int32) + place[0] * (GRID // 2), GRID).astype(F32)
    below = 2.0 * (line + 0.5) / GRID - 1.0
    pa = across[:, None] * along[None, :]
    pb = below[:, None] * down[None, :]
    tables = (jnp.sin(pa), jnp.cos(pa), jnp.sin(pb), jnp.cos(pb))
    ready = prep(peer, HALF, *tables, filled=prep(own, 0, *tables))
    pe = token_pe(coords)
    q0 = by_token(queries.astype(F32))
    cq = by_token(cot_q.astype(F32))
    place, ready, pe, q0, cq, mine = lax.optimization_barrier((place, ready, pe, q0, cq, mine))
    k0, lh, ll, lht, llt, k0t = ready
    s1, big, a32, b32, w16, slim, wself = tokens(place, q0, pe, mine, swap(mine), lh, ll, k0t)
    keys, img, one, two, three, c32 = image_side(
        place, cot_k, k0, lh, ll, lht, llt, s1, big, cq, a32, b32, w16, slim
    )
    parts = one, two, three
    gmine, gother, dq = param_grads(place, pe, a32, b32, slim, c32, wself)
    queries_out = a32[TOK2 + 96 : TOK2 + 128]
    return by_box(queries_out).astype(BF), keys, by_box(dq), img, parts, gmine, gother


SWAP = [(0, 1), (1, 0)]
HALFWAY = ("cuts_0", "cuts_1", "cuts_2", "box")
RING_Y = ("cuts_1", "box")


def passed(x, axis, step):
    return lax.ppermute(x, axis, [(i, (i + step) % 4) for i in range(4)])


def ring_all(x, axis):
    return [x, passed(x, axis, 1), passed(x, axis, -1), passed(x, axis, 2)]


def swap(x):
    return lax.ppermute(x, "cuts_3", SWAP)


def local(
    queries_in, image, box_coords, box_mask, volume_ids, cot_queries, cot_keys, master, moment1, moment2,
):
    box = lax.axis_index("box")
    me = lax.axis_index(CUTS_BOX)
    own = image[0]
    shard = master.shape[0]
    first_row = ((771 * me) // 64) * 8
    shift = shard * me - 128 * first_row
    peer = lax.ppermute(own, "box", SWAP)
    room = 1024
    long = jnp.concatenate(
        [jnp.zeros((room,), BF), master.astype(BF), jnp.zeros((CHUNK * 128 - shard,), BF)]
    )
    chunk = lax.dynamic_slice(long, (room - shift,), (CHUNK * 128,)).reshape(CHUNK, 128)
    last = jnp.concatenate([box_mask[0].astype(BF), volume_ids.astype(BF), jnp.zeros((123,), BF)])
    chunk = jnp.where(jnp.arange(CHUNK, dtype=jnp.int32)[:, None] == CHUNK - 1, last[None], chunk)
    column = jnp.stack(ring_all(chunk, RING_Y))
    plane = lax.all_to_all(
        jnp.broadcast_to(column[None], (PEERS // 4, 4, CHUNK, 128)), ("cuts_0", "cuts_2"), 0, 0, tiled=True
    )
    mine = plane.reshape(PEERS, CHUNK, 128)
    place = jnp.concatenate(
        [
            jnp.stack([box, lax.axis_index("cuts_3"), 2 * lax.axis_index("cuts_1") + box, volume_ids[0]]),
            box_mask[0],
        ]
    ).astype(jnp.int32)

    queries_out, keys_out, queries_grad, img, parts, gmine, gother = device_work(
        place, own, peer, queries_in[0], box_coords[0], cot_queries[0], cot_keys[0], mine, swap
    )
    one, two, three = parts
    one = lax.ppermute(one, "box", SWAP)
    gother, one, two = lax.optimization_barrier((gother, one, two))
    two = lax.ppermute(two, "box", SWAP)

    start = shard * me
    edges = jnp.array([128 * r for r in ROW0[1:]], jnp.int32)
    piece = jnp.sum((edges <= start).astype(jnp.int32))
    edge = functools.reduce(
        lambda e, r: jnp.where((128 * r > start) & (e > 128 * r), 128 * r, e), ROW0[1:], start + shard
    )
    cut = jnp.minimum(edge, start + shard) - start

    def laid(x):
        return lax.dynamic_update_slice(jnp.zeros((CHUNK * 128,), F32), x, (shift,)).reshape(CHUNK, 128)

    def taken(x):
        return lax.dynamic_slice(x.reshape(CHUNK * 128), (shift,), (shard,))

    states = [laid(x) for x in (master, moment1, moment2)]
    sent = merge(gmine, swap(gother))
    sent, two, img = lax.optimization_barrier((sent, two, img))
    came = lax.all_to_all(sent, HALFWAY, 0, 0, tiled=True)
    img = land(land(img, one, PART0[0]), two, PART0[1])
    where = jnp.stack([shift, shift + cut, shift + shard, piece]).astype(jnp.int32)
    came, three, img, states, where = lax.optimization_barrier((came, three, img, states, where))
    three = lax.ppermute(three, "box", SWAP)
    new_first, new_second, update, squares = settle(where, came, *states)
    squares = lax.all_to_all(squares, CUTS_BOX, 0, 0, tiled=True)
    new_first, new_second, update = taken(new_first), taken(new_second), taken(update)
    image_grad = land(img, three, PART0[2])
    squares, image_grad = lax.optimization_barrier((squares, image_grad))
    squares = jnp.sum(squares, axis=(0, 1))
    weight_norm = jnp.sqrt(squares[:14])
    update_norm = jnp.sqrt(squares[64:78])
    ratio = jnp.concatenate([weight_norm / (update_norm + 1e-06), jnp.ones((2,), F32)])
    entry = jnp.where(jnp.arange(shard, dtype=jnp.int32) < cut, ratio[piece], ratio[piece + 1])
    new_master = master - 0.25 * entry * update
    return (
        queries_out[None],
        keys_out[None],
        queries_grad[None],
        image_grad[None],
        new_master,
        new_first,
        new_second,
        new_master.astype(BF),
        jnp.stack([weight_norm, update_norm]),
    )


def solution(mesh):
    torus = Mesh(
        mesh.devices.reshape(4, 2, 4, 2, mesh.shape["box"]),
        ("cuts_0", "cuts_1", "cuts_2", "cuts_3", "box"),
    )
    in_specs = (
        P(CUTS, "box", None, None),
        P(CUTS, "box", None),
        P(CUTS, "box", None),
        P(CUTS, "box"),
        P(CUTS),
        P(CUTS, "box", None, None),
        P(CUTS, "box", None, None),
        P(CUTS_BOX),
        P(CUTS_BOX),
        P(CUTS_BOX),
    )
    out_specs = (
        P(CUTS, "box", None, None),
        P(CUTS, "box", None, None),
        P(CUTS, "box", None, None),
        P(CUTS, "box", None),
        P(CUTS_BOX),
        P(CUTS_BOX),
        P(CUTS_BOX),
        P(CUTS_BOX),
        P(),
    )
    return jax.shard_map(local, mesh=torus, in_specs=in_specs, out_specs=out_specs, check_vma=False)
```
